512 devices in a mesh: outer: 32 (over z, x_hi, core), chip: 16 (over y, x_lo).
Axes of the slice: x: 4 (x_hi: 2, x_lo: 2; x = x_hi * 2 + x_lo), y: 8, z: 8, core: 2. Of those that a mesh axis runs over, the one named last changes fastest.
Arguments:
- hidden: bfloat16 [64, 256, 2048], P('outer', 'chip'), may hold values from -6 to 6
- down_weight: bfloat16 [64, 2048, 7168], P('outer', None, 'chip'), may hold values from -0.125 to 0.125
- out_grad: bfloat16 [1536, 7168], P('outer', 'chip'), may hold values from -6 to 6
- routes: int32 [1536, 8], P('outer'), may hold values from 0 to 63, as said below
- gates: float32 [1536, 8], P('outer'), may hold values from 0.1 to 0.6
- omega: float32 [7168, 32], P('chip'), may hold values from -0.0625 to 0.0625
- psi: float32 [2048, 32], replicated, may hold values from -0.125 to 0.125
- left_old: float32 [64, 2048, 32], P('outer', 'chip'), may hold values from -6 to 6
- right_old: float32 [64, 7168, 32], P('outer', 'chip'), may hold values from -6 to 6
- moves: int32 [4, 2], replicated, may hold values from 0 to 31, as said below
Outputs:
- mixed: bfloat16 [1536, 7168], P('outer', 'chip')
- hidden_grad: bfloat16 [64, 256, 2048], P('outer', 'chip')
- left_moved: float32 [64, 2048, 32], P('outer', 'chip')
- right_moved: float32 [64, 7168, 32], P('outer', 'chip')
The draws below stay inside these ranges and needn't reach their ends.
Inputs may be any that keep to these rules, and one draw needn't show every extreme that they name: `routes`: each row names 8 different experts, all of them in at most 4 pods, where pod q holds the experts 2 * 2 * q to 2 * 2 * (q + 1) - 1. `moves`: the 8 entries are different groups. In some row the two groups are 16 apart, and in some other row they are neighbours (index difference 1).
All inputs are finite; a program needn't handle non-finite values.
Results may differ from the reference program's by a relative error of at most 0.022.
Values may be sent and summed in bfloat16 or wider, within the bound.
A program may use at most 64 MiB of HBM per device.

```python
import math
import jax
import jax.numpy as jnp
from jax import lax

D = 7168
FF = 2048
TOP = 8
EXP_OUT = 2
POD_LIMIT = 4
RANK = 32
MOVES = 4
TOK_OUT = 48
SLOT = 8
EROWS = 256
EXPERTS = 64
TOKENS = 1536
N_OUTER = 32
N_CHIP = 16


def draw_routes(key, part):
    key = jax.random.fold_in(key, 11)
    pod_total = N_OUTER // 2
    per_pod = 2 * EXP_OUT
    key_one, key_two, key_three, key_four = jax.random.split(key, 4)
    pod_bias = jax.random.randint(key_one, (pod_total,), 0, 3) * 2 ** 16
    pod_score = jax.random.randint(key_two, (TOKENS, pod_total), 0, 2 ** 18) + pod_bias[None, :]
    pod_score = pod_score * pod_total + jnp.arange(pod_total, dtype=jnp.int32)[None, :]
    unused, chosen = lax.top_k(pod_score, POD_LIMIT)
    candidates = (chosen[:, :, None] * per_pod + jnp.arange(per_pod, dtype=jnp.int32)[None, None, :]).reshape(TOKENS, POD_LIMIT * per_pod)
    expert_bias = jax.random.randint(key_three, (EXPERTS,), 0, 3) * 2 ** 16
    cand_score = jax.random.randint(key_four, (TOKENS, POD_LIMIT * per_pod), 0, 2 ** 18) + expert_bias[candidates]
    cand_score = cand_score * (POD_LIMIT * per_pod) + jnp.arange(POD_LIMIT * per_pod, dtype=jnp.int32)[None, :]
    unused_two, picked = lax.top_k(cand_score, TOP)
    return jnp.take_along_axis(candidates, picked, axis=1).astype(jnp.int32)


def draw_moves(key, part):
    key = jax.random.fold_in(key, 23)
    key_one, key_two, key_three = jax.random.split(key, 3)
    half = N_OUTER // 2
    first = jnp.int32(0)
    across = jnp.int32(half)
    near_one = jnp.int32(N_OUTER - 2)
    near_two = jnp.int32(N_OUTER - 1)
    groups = jnp.arange(N_OUTER, dtype=jnp.int32)
    used = (groups == first) | (groups == across) | (groups == near_one) | (groups == near_two)
    scores = jax.random.randint(key_one, (N_OUTER,), 0, 2 ** 20) * N_OUTER + groups
    scores = jnp.where(used, -1, scores)
    unused, others = lax.top_k(scores, 2 * (MOVES - 2))
    fixed_pairs = jnp.stack([jnp.stack([first, across]), jnp.stack([near_one, near_two])])
    all_pairs = jnp.concatenate([fixed_pairs, others.astype(jnp.int32).reshape(MOVES - 2, 2)], axis=0)
    flips = jax.random.randint(key_two, (MOVES, 1), 0, 2)
    all_pairs = jnp.where(flips == 1, all_pairs[:, ::-1], all_pairs)
    order = jax.random.permutation(key_three, MOVES)
    return all_pairs[order].astype(jnp.int32)


def steps_of(stream_key, extent, pieces, low, largest):
    def one(position, blocks):
        steps = jax.random.uniform(jax.random.fold_in(jax.random.fold_in(stream_key, 6), position), (blocks,), jnp.float32, low / len(pieces), largest / len(pieces))
        return jnp.repeat(jnp.exp(steps), extent[position] // blocks).reshape((-1,) + (1,) * (len(extent) - position - 1))

    loudness = one(*pieces[0])
    for cut in pieces[1:]:
        loudness = loudness * one(*cut)
    return loudness


def bell_draw(stream_key, dims, spread, limit, pieces=(), kind=jnp.bfloat16):
    drawn = jax.random.normal(stream_key, dims, jnp.float32) * spread
    if len(pieces) > 0:
        drawn = steps_of(stream_key, dims, pieces, -0.22, 0.18) * drawn
    return jnp.clip(drawn, min=-limit, max=limit).astype(kind)


def setup_inputs(seed: int = 0) -> dict:
    arg_keys = jax.random.split(jax.random.key(seed), 11)
    hidden = bell_draw(arg_keys[0], (EXPERTS, EROWS, FF), 1.0, 6.0, ((0, 32), (1, 16)))
    down_weight = bell_draw(arg_keys[1], (EXPERTS, FF, D), FF ** -0.5, 0.125, ((0, 32), (2, 16)))
    out_grad = bell_draw(arg_keys[2], (TOKENS, D), 1.0, 6.0, ((0, 32), (1, 16)))
    routes = draw_routes(jax.random.fold_in(arg_keys[10], 71), 0)
    gates = jnp.clip(0.1 + 0.5 * jax.random.uniform(arg_keys[4], (TOKENS, TOP), jnp.float32) ** steps_of(arg_keys[4], (TOKENS, TOP), ((0, 32),), -0.2, 0.2), 0.1, 0.6)
    omega = bell_draw(arg_keys[5], (D, RANK), D ** -0.5, 0.0625, ((0, 16),), jnp.float32)
    psi = bell_draw(arg_keys[6], (FF, RANK), FF ** -0.5, 0.125, (), jnp.float32)
    left_old = bell_draw(arg_keys[7], (EXPERTS, FF, RANK), 1.0, 6.0, ((0, 32), (1, 16)), jnp.float32)
    right_old = bell_draw(arg_keys[8], (EXPERTS, D, RANK), 1.0, 6.0, ((0, 32), (1, 16)), jnp.float32)
    moves = draw_moves(jax.random.fold_in(arg_keys[10], 71), 0)
    return dict(hidden=hidden, down_weight=down_weight, out_grad=out_grad, routes=routes, gates=gates, omega=omega, psi=psi, left_old=left_old, right_old=right_old, moves=moves)


highest = lax.Precision.HIGHEST

def slot_places(routes):
    pair_rows = routes.reshape(N_OUTER, TOK_OUT * TOP)
    expert_ids = jnp.arange(EXPERTS, dtype=jnp.int32)
    onehot = (pair_rows[:, :, None] == expert_ids[None, None, :]).astype(jnp.int32)
    earlier = jnp.cumsum(onehot, axis=1) - onehot
    rank_of = lax.optimization_barrier(jnp.sum(earlier * onehot, axis=2))
    source_ids = jnp.arange(N_OUTER, dtype=jnp.int32)[:, None]
    places = pair_rows * EROWS + source_ids * SLOT + jnp.minimum(rank_of, SLOT - 1)
    return (places.reshape(TOKENS, TOP).astype(jnp.int32), (rank_of < SLOT).reshape(TOKENS, TOP))

def reference(hidden, down_weight, out_grad, routes, gates, omega, psi, left_old, right_old, moves):
    places, kept = slot_places(routes)
    pair_weight = jnp.where(kept, gates, 0.0).astype(jnp.float32)

    def project(items):
        return jnp.einsum('rf,fd->rd', items[0].astype(jnp.float32), items[1].astype(jnp.float32), precision=highest).astype(jnp.bfloat16)
    expert_out = lax.map(project, (hidden, down_weight)).reshape(EXPERTS * EROWS, D)
    picked = expert_out[places.reshape(-1)].reshape(TOKENS, TOP, D).astype(jnp.float32)
    mixed = jnp.einsum('tp,tpd->td', pair_weight, picked, precision=highest).astype(jnp.bfloat16)
    scaled = pair_weight[:, :, None] * out_grad.astype(jnp.float32)[:, None, :]
    routed = jnp.zeros((EXPERTS * EROWS, D), jnp.float32).at[places.reshape(-1)].add(scaled.reshape(TOKENS * TOP, D))
    expert_grad = routed.astype(jnp.bfloat16).reshape(EXPERTS, EROWS, D)
    scale_right = 10.0 / (EROWS * (FF / math.sqrt(D) + math.sqrt(FF)))
    scale_left = 10.0 / (EROWS * (D / math.sqrt(FF) + math.sqrt(D)))

    def per_expert(items):
        rows_in, weight_in, grad_in, left_in, right_in = items
        rows_wide = rows_in.astype(jnp.float32)
        weight_wide = weight_in.astype(jnp.float32)
        grad_wide = grad_in.astype(jnp.float32)
        partial_value = jnp.einsum('rcd,fcd->crf', grad_wide.reshape(EROWS, N_CHIP, D // N_CHIP), weight_wide.reshape(FF, N_CHIP, D // N_CHIP), precision=highest)
        rounded = lax.optimization_barrier(partial_value.astype(jnp.bfloat16))
        grad_hidden = lax.optimization_barrier(jnp.sum(rounded.astype(jnp.float32), axis=0)).astype(jnp.bfloat16)
        weight_grad = jnp.einsum('rf,rd->fd', rows_wide, grad_wide, precision=highest)
        sketch_cols = jnp.dot(weight_grad, omega, precision=highest)
        right_new = 0.5 * right_in + 0.5 * scale_right * jnp.dot(weight_grad.T, sketch_cols, precision=highest)
        sketch_rows = jnp.dot(weight_grad.T, psi, precision=highest)
        left_new = 0.5 * left_in + 0.5 * scale_left * jnp.dot(weight_grad, sketch_rows, precision=highest)
        return (grad_hidden, left_new, right_new)
    hidden_grad, left_new, right_new = lax.map(per_expert, (hidden, down_weight, expert_grad, left_old, right_old))
    positions = jnp.arange(N_OUTER, dtype=jnp.int32)
    source = positions
    for move_index in range(MOVES):
        from_group = moves[move_index, 0]
        to_group = moves[move_index, 1]
        source = jnp.where(positions == from_group, to_group, jnp.where(positions == to_group, from_group, source))
    source_expert = (source[:, None] * EXP_OUT + jnp.arange(EXP_OUT, dtype=jnp.int32)[None, :]).reshape(-1)
    return (mixed, hidden_grad, left_new[source_expert], right_new[source_expert])
```

```python
import math

import jax
import jax.numpy as jnp
from jax import lax
from jax.sharding import PartitionSpec as P

highest = lax.Precision.HIGHEST


def broadcast(shard, axis, root):
    mine = lax.axis_index(axis) == root
    return lax.psum(jnp.where(mine, shard, jnp.zeros_like(shard)), axis)


def on_device(hidden, down_weight, out_grad, routes, gates, omega, psi, left_old, right_old, moves):
    outer_size = lax.axis_size("outer")
    chip_size = lax.axis_size("chip")
    local_experts = down_weight.shape[0]
    hidden_width = down_weight.shape[1]
    column_count = down_weight.shape[2]
    model_width = column_count * chip_size
    token_rows = routes.shape[0]
    pick_count = routes.shape[1]
    expert_rows = hidden.shape[1] * chip_size
    slot_count = expert_rows // outer_size
    all_experts = local_experts * outer_size
    buffer_rows = all_experts * slot_count
    pair_ids = routes.reshape(-1)
    onehot = (pair_ids[:, None] == jnp.arange(all_experts, dtype=jnp.int32)[None, :]).astype(
        jnp.int32
    )
    earlier = jnp.cumsum(onehot, axis=0) - onehot
    rank_of = jnp.sum(earlier * onehot, axis=1)
    local_index = pair_ids % local_experts
    group_index = pair_ids // local_experts
    buffer_index = local_index * expert_rows + group_index * slot_count + rank_of
    buffer_index = jnp.where(rank_of < slot_count, buffer_index, -1)
    matches = (buffer_index[:, None] == jnp.arange(buffer_rows, dtype=jnp.int32)[None, :]).astype(
        jnp.float32
    )
    weighted = matches * gates.reshape(-1)[:, None]
    assign = jnp.sum(weighted.reshape(token_rows, pick_count, buffer_rows), axis=1)
    outgoing = jnp.dot(assign.T, out_grad.astype(jnp.float32), precision=highest).astype(
        jnp.bfloat16
    )
    outgoing = outgoing.reshape(local_experts, outer_size, slot_count, column_count)
    expert_grad = lax.all_to_all(
        outgoing, "outer", split_axis=1, concat_axis=1, tiled=True
    ).reshape(local_experts, expert_rows, column_count)
    full_rows = lax.all_gather(hidden, "chip", axis=1, tiled=True)
    expert_out = jnp.einsum(
        "kmf,kfd->kmd", full_rows, down_weight, preferred_element_type=jnp.float32
    ).astype(jnp.bfloat16)
    returned = lax.all_to_all(
        expert_out.reshape(local_experts, outer_size, slot_count, column_count),
        "outer",
        split_axis=1,
        concat_axis=1,
        tiled=True,
    )
    mixed = jnp.dot(
        assign, returned.reshape(buffer_rows, column_count).astype(jnp.float32), precision=highest
    ).astype(jnp.bfloat16)
    partial_value = jnp.einsum(
        "kmd,kfd->kmf", expert_grad, down_weight, preferred_element_type=jnp.float32
    )
    hidden_grad = lax.psum_scatter(
        partial_value.astype(jnp.bfloat16), "chip", scatter_dimension=1, tiled=True
    )
    scale_right = 10.0 / (
        expert_rows * (hidden_width / math.sqrt(model_width) + math.sqrt(hidden_width))
    )
    scale_left = 10.0 / (
        expert_rows * (model_width / math.sqrt(hidden_width) + math.sqrt(model_width))
    )
    wide_rows = full_rows.astype(jnp.float32)
    wide_grad = expert_grad.astype(jnp.float32)
    row_cols = lax.psum(jnp.einsum("kmd,dr->kmr", wide_grad, omega, precision=highest), "chip")
    sketch_cols = jnp.einsum("kmf,kmr->kfr", wide_rows, row_cols, precision=highest)
    row_width = jnp.einsum("kmf,kfr->kmr", wide_rows, sketch_cols, precision=highest)
    right_step = jnp.einsum("kmd,kmr->kdr", wide_grad, row_width, precision=highest)
    row_psi = jnp.einsum("kmf,fr->kmr", wide_rows, psi, precision=highest)
    width_side = jnp.einsum("kmd,kmr->kdr", wide_grad, row_psi, precision=highest)
    row_left = lax.psum(jnp.einsum("kmd,kdr->kmr", wide_grad, width_side, precision=highest), "chip")
    own = hidden_width // chip_size
    own_rows = lax.dynamic_slice_in_dim(wide_rows, lax.axis_index("chip") * own, own, 2)
    left_step = jnp.einsum("kmf,kmr->kfr", own_rows, row_left, precision=highest)
    right_new = 0.5 * right_old + 0.5 * scale_right * right_step
    left_new = 0.5 * left_old + 0.5 * scale_left * left_step
    outer_index = lax.axis_index("outer")
    source = outer_index
    for move_index in range(moves.shape[0]):
        from_group = moves[move_index, 0]
        to_group = moves[move_index, 1]
        source = jnp.where(
            outer_index == from_group,
            to_group,
            jnp.where(outer_index == to_group, from_group, source),
        )
    payload = jnp.concatenate([left_new, right_new], axis=1).astype(jnp.bfloat16)
    payload = payload.reshape(-1, 128)
    gathered = lax.all_gather(payload, "outer", axis=0, tiled=False)
    arrived = lax.dynamic_index_in_dim(gathered, source, 0, keepdims=False)
    arrived = arrived.reshape(local_experts, own + column_count, -1).astype(jnp.float32)
    stays = source == outer_index
    left_moved = jnp.where(stays, left_new, arrived[:, :own])
    right_moved = jnp.where(stays, right_new, arrived[:, own:])
    return (mixed, hidden_grad, left_moved, right_moved)


def solution(mesh):
    in_specs = (
        P("outer", "chip", None),
        P("outer", None, "chip"),
        P("outer", "chip"),
        P("outer", None),
        P("outer", None),
        P("chip", None),
        P(),
        P("outer", "chip", None),
        P("outer", "chip", None),
        P(),
    )
    out_specs = (
        P("outer", "chip"),
        P("outer", "chip", None),
        P("outer", "chip", None),
        P("outer", "chip", None),
    )
    return jax.shard_map(
        on_device, mesh=mesh, in_specs=in_specs, out_specs=out_specs, check_vma=False
    )
```

```python
import functools
import math

import jax
import jax.numpy as jnp
from jax import lax
from jax.experimental import pallas as pl
from jax.experimental.pallas import tpu as pltpu
from jax.sharding import PartitionSpec as P

MESH = pl.DeviceIdType.MESH
WAY = (1, -1)


def dot(a, b, a_dim, b_dim):
    return lax.dot_general(
        a, b, (((a_dim,), (b_dim,)), ((), ())), preferred_element_type=jnp.float32
    )


def halves(a):
    high = a.astype(jnp.bfloat16)
    return high, (a - high.astype(jnp.float32)).astype(jnp.bfloat16)


def dot_halves(a, b, b_dim):
    high, low = halves(a)
    both = dot(jnp.concatenate([high, low], axis=0), b, 1, b_dim)
    return both[: a.shape[0]] + both[a.shape[0] :]


def kernel(
    sizes,
    hid, wt, og, routes, gates, om, ps, left_old, right_old, moves,
    mixed, hidden_grad, left_out, right_out,
    full, wv, assign, ob, gb, grad, part, rs_in, x_in, eo, rb,
    us, ui, uo, ua, vs, vi, vo, va, rn, ln, pay, tz, sel, t2,
    w_sem, ag_s, ag_r, agx_s, agx_r, rs_s, rs_r, rsx_s, rsx_r, one_s, one_r,
):
    outer_size, chip_size, zn, yn, scale_left, scale_right = sizes
    o, c = lax.axis_index("outer"), lax.axis_index("chip")
    z, sub = o // 4, o % 4
    y, xl = c // 2, c % 2
    experts, block, hidden_width = hid.shape
    columns = og.shape[1]
    rank = om.shape[0]
    rows_all = full.shape[1]
    own = left_old.shape[2]
    steps = yn - 1

    barrier = pltpu.get_barrier_semaphore()

    @pl.loop(1, outer_size)
    def _(i):
        pl.semaphore_signal(barrier, inc=1, device_id=((o + i) % outer_size, c), device_id_type=MESH)

    @pl.loop(1, chip_size)
    def _(i):
        pl.semaphore_signal(barrier, inc=1, device_id=(o, (c + i) % chip_size), device_id_type=MESH)

    w_copy = pltpu.make_async_copy(wt, wv, w_sem)
    w_copy.start()

    routes_now, gates_now = routes[...], gates[...]
    tokens = routes_now.shape[1]
    place = lax.broadcasted_iota(jnp.int32, assign.shape, 0)
    expert = lax.shift_right_logical(place, 3)
    slot = (place & 7).astype(jnp.float32)
    picked = jnp.zeros(assign.shape, jnp.float32)
    weight = jnp.zeros(assign.shape, jnp.float32)
    for p in range(routes_now.shape[0]):
        hit = routes_now[p : p + 1, :] == expert
        picked = picked + jnp.where(hit, 1.0, 0.0)
        weight = weight + jnp.where(hit, gates_now[p : p + 1, :], 0.0)
    earlier = lax.broadcasted_iota(jnp.int32, (tokens, tokens), 0) < lax.broadcasted_iota(
        jnp.int32, (tokens, tokens), 1
    )
    ranks = dot(picked.astype(jnp.bfloat16), jnp.where(earlier, 1.0, 0.0).astype(jnp.bfloat16), 1, 0)
    weight = jnp.where(ranks == slot, weight, 0.0)
    assign[...] = weight
    high, low = halves(weight)
    og_now = og[...]
    outgoing = dot(high, og_now, 1, 0) + dot(low, og_now, 1, 0)
    ob[...] = outgoing.astype(jnp.bfloat16).reshape(ob.shape)
    gb[o] = ob[o]

    def rows(chip):
        return pl.ds(pl.multiple_of(chip * block, block), block)

    for k in range(experts):
        full[k, rows(c), :] = hid[k]

    pl.semaphore_wait(barrier, outer_size + chip_size - 2)

    def remote(src, dst, send, recv, device):
        return pltpu.make_async_remote_copy(
            src_ref=src, dst_ref=dst, send_sem=send, recv_sem=recv, device_id=device, device_id_type=MESH
        )

    def along_y(k):
        return (o, ((y + WAY[k] + yn) % yn) * 2 + xl)

    x_partner = (o, 2 * y + 1 - xl)

    def ag_copy(k, s, j):
        source = 2 * ((y - WAY[k] * s + yn) % yn) + (xl if j == 0 else 1 - xl)
        src = hid.at[k] if s == 0 and j == 0 else full.at[k, rows(source)]
        return remote(src, full.at[k, rows(source)], ag_s.at[k, s, j], ag_r.at[k, s, j], along_y(k))

    def ag_x(k):
        return remote(hid.at[k], full.at[k, rows(c)], agx_s.at[k], agx_r.at[k], x_partner)

    def ag_step(s):
        for j in range(2):
            for k in range(experts):
                ag_copy(k, s, j).wait_recv()
                if s + 1 < steps:
                    ag_copy(k, s + 1, j).start()

    for k in range(experts):
        ag_x(k).start()
        ag_copy(k, 0, 0).start()

    def spread(src_of, dst, number, axis_size, device_of):
        @pl.loop(1, axis_size)
        def _(i):
            remote(src_of(i), dst, one_s.at[number], one_r.at[number], device_of(i)).start()

    def arrived(buf, count, number):
        ref = buf.at[pl.ds(0, count)]
        pltpu.make_async_copy(ref, ref, one_r.at[number]).wait()

    def sent(buf, count, number):
        ref = buf.at[pl.ds(0, count)]
        pltpu.make_async_copy(ref, ref, one_s.at[number]).wait()

    def other_group(i):
        return (o + i) % outer_size

    def other_chip(i):
        return (c + i) % chip_size

    spread(lambda i: ob.at[other_group(i)], gb.at[o], 0, outer_size, lambda i: (other_group(i), c))

    for k in range(experts):
        ag_x(k).wait_recv()
        ag_copy(k, 0, 1).start()

    early = min(3, steps - 1)
    for s in range(early):
        ag_step(s)

    arrived(gb, outer_size - 1, 0)
    eight = block // experts
    come = gb[...].astype(jnp.float32)
    for k in range(experts):
        grad[k] = come[:, k * eight : (k + 1) * eight, :].reshape(rows_all, columns).astype(jnp.bfloat16)

    lanes = us.shape[2]
    lane_cuts = rows_all // lanes
    piece = us.shape[1]

    def sum_send(parts, send, into, number):
        both = jnp.concatenate(parts, axis=0)
        for p in range(chip_size):
            at, cut = p // lane_cuts, p % lane_cuts
            send[p] = both[at * piece : (at + 1) * piece, cut * lanes : (cut + 1) * lanes]
        into[c] = send[c]
        spread(lambda i: send.at[other_chip(i)], into.at[c], number, chip_size, lambda i: (o, other_chip(i)))

    def sum_share(into, own_sum, full_sum, number):
        arrived(into, chip_size - 1, number)
        own_sum[...] = jnp.sum(into[...], axis=0)
        full_sum[c] = own_sum[...]
        spread(lambda i: own_sum, full_sum.at[c], number + 1, chip_size, lambda i: (o, other_chip(i)))

    def sum_take(full_sum, number):
        arrived(full_sum, chip_size - 1, number + 1)
        lines = []
        for at in range(chip_size // lane_cuts):
            lines.append(
                jnp.concatenate([full_sum[at * lane_cuts + cut] for cut in range(lane_cuts)], axis=1)
            )
        both = jnp.concatenate(lines, axis=0)
        return [both[k * rank : (k + 1) * rank] for k in range(experts)]

    omega = om[...]
    sum_send([dot_halves(omega, grad[k], 1) for k in range(experts)], us, ui, 1)

    w_copy.wait()
    tile = min(512, hidden_width)

    def partial_of(k):
        @pl.loop(0, hidden_width // tile)
        def _(n):
            cut = pl.ds(pl.multiple_of(n * tile, tile), tile)
            part[k, :, cut] = dot(grad[k], wv[k, :, cut], 1, 0).astype(jnp.bfloat16)

    partial_of(0)
    ag_step(early)
    partial_of(1)
    for s in range(early + 1, steps):
        ag_step(s)

    def rs_rows(k, s, j):
        return rows(2 * ((y - WAY[k] * (s + 1) + 2 * yn) % yn) + (1 - xl if j == 0 else xl))

    def rs_copy(k, s, j):
        return remote(
            part.at[k, rs_rows(k, s, j)], rs_in.at[k, s, j], rs_s.at[k, s, j], rs_r.at[k, s, j], along_y(k)
        )

    def rs_add(k, s, j):
        rs_copy(k, s - 1, j).wait_recv()
        return part[k, rs_rows(k, s, j), :].astype(jnp.float32) + rs_in[k, s - 1, j].astype(jnp.float32)

    def rs_step(s):
        for j in range(2):
            for k in range(experts):
                part[k, rs_rows(k, s, j), :] = rs_add(k, s, j).astype(jnp.bfloat16)
                rs_copy(k, s, j).start()

    def rs_x(k):
        return remote(part.at[k, rs_rows(k, steps, 0)], x_in.at[k], rsx_s.at[k], rsx_r.at[k], x_partner)

    for j in range(2):
        for k in range(experts):
            rs_copy(k, 0, j).start()

    todo = list(range(1, steps))

    def rs_next():
        if todo:
            rs_step(todo.pop(0))

    width = ps[...]
    left_parts = []
    for k in range(experts):
        row_psi = dot_halves(width, full[k], 1)
        width_side = dot_halves(row_psi, grad[k], 0)
        left_parts.append(dot_halves(width_side, grad[k], 1))
    sum_send(left_parts, vs, vi, 3)
    sum_share(ui, uo, ua, 1)

    outputs = []
    for k in range(experts):
        outputs.append(dot(full[k], wv[k], 1, 1).reshape(outer_size, eight, columns))
        if k == 0:
            rs_next()
    eo[...] = jnp.concatenate(outputs, axis=1).astype(jnp.bfloat16)
    rb[o] = eo[o]
    spread(lambda i: eo.at[other_group(i)], rb.at[o], 5, outer_size, lambda i: (other_group(i), c))
    sum_share(vi, vo, va, 3)
    rs_next()

    row_cols = sum_take(ua, 1)
    for k in range(experts):
        sketch = dot_halves(row_cols[k], full[k], 0)
        row_width = dot_halves(sketch, full[k], 1)
        rn[k] = 0.5 * right_old[k] + 0.5 * scale_right * dot_halves(row_width, grad[k], 0)
    rs_next()
    row_left = sum_take(va, 3)
    mine = pl.ds(pl.multiple_of(c * own, own), own)
    for k in range(experts):
        ln[k] = 0.5 * left_old[k] + 0.5 * scale_left * dot_halves(row_left[k], full[k, :, mine], 0)

    for k in range(experts):
        pay[:, k * columns : (k + 1) * columns] = rn[k].astype(jnp.bfloat16)
        at = experts * columns + k * own
        pay[:, at : at + own] = ln[k].astype(jnp.bfloat16)
    tz[z] = pay[...]
    spread(lambda i: pay, tz.at[z], 6, zn, lambda i: (((z + i) % zn) * 4 + sub, c))

    def source_of(group):
        source = group
        for m in range(moves.shape[0]):
            a, b = moves[m, 0], moves[m, 1]
            source = jnp.where(group == a, b, jnp.where(group == b, a, source))
        return source

    for _ in range(2):
        rs_next()

    arrived(rb, outer_size - 1, 5)
    back = rb[...].reshape(outer_size * block, columns)
    high, low = halves(assign[...])
    mixed[...] = (dot(high, back, 0, 0) + dot(low, back, 0, 0)).astype(jnp.bfloat16)

    while todo:
        rs_next()

    arrived(tz, zn - 1, 6)
    for i in range(1, 4):
        sel[i - 1] = tz[lax.shift_right_logical(source_of(z * 4 + (sub + i) % 4), 2)]
        remote(
            sel.at[i - 1], t2.at[sub], one_s.at[7], one_r.at[7], (z * 4 + (sub + i) % 4, c)
        ).start()

    for k in range(experts):
        part[k, rs_rows(k, steps, 0), :] = rs_add(k, steps, 0).astype(jnp.bfloat16)
        rs_x(k).start()
    for k in range(experts):
        total = rs_add(k, steps, 1)
        rs_x(k).wait_recv()
        hidden_grad[k] = (total + x_in[k].astype(jnp.float32)).astype(jnp.bfloat16)

    mine_from = source_of(o)
    stays = mine_from == o
    arrived(t2, 3, 7)
    t2[sub] = tz[lax.shift_right_logical(mine_from, 2)]
    came = t2[mine_from & 3].astype(jnp.float32)
    for k in range(experts):
        right_out[k] = jnp.where(stays, rn[k], came[:, k * columns : (k + 1) * columns])
        at = experts * columns + k * own
        left_out[k] = jnp.where(stays, ln[k], came[:, at : at + own])

    for k in range(experts):
        ag_x(k).wait_send()
        rs_x(k).wait_send()
        for s in range(steps):
            for j in range(2):
                ag_copy(k, s, j).wait_send()
                rs_copy(k, s, j).wait_send()
    sent(ob, outer_size - 1, 0)
    sent(us, chip_size - 1, 1)
    sent(ua, chip_size - 1, 2)
    sent(vs, chip_size - 1, 3)
    sent(va, chip_size - 1, 4)
    sent(eo, outer_size - 1, 5)
    sent(tz, zn - 1, 6)
    sent(sel, 3, 7)


def on_device(hidden, down_weight, out_grad, routes, gates, omega, psi, left_old, right_old, moves):
    outer_size = lax.axis_size("outer")
    chip_size = lax.axis_size("chip")
    experts, hidden_width, columns = down_weight.shape
    model_width = columns * chip_size
    block = hidden.shape[1]
    rows_all = block * chip_size
    own = left_old.shape[1]
    rank = omega.shape[1]
    tokens = routes.shape[0]
    zn, yn = outer_size // 4, chip_size // 2
    scale_right = 10.0 / (rows_all * (hidden_width / math.sqrt(model_width) + math.sqrt(hidden_width)))
    scale_left = 10.0 / (rows_all * (model_width / math.sqrt(hidden_width) + math.sqrt(model_width)))
    lanes = min(rows_all, 128)
    piece = experts * rank * (rows_all // lanes) // chip_size
    pay_width = experts * (columns + own)
    bf16, f32 = jnp.bfloat16, jnp.float32
    dma = pltpu.SemaphoreType.DMA
    vmem = pl.BlockSpec(memory_space=pltpu.VMEM)
    mixed, hidden_grad, left_moved, right_moved = pl.pallas_call(
        functools.partial(kernel, (outer_size, chip_size, zn, yn, scale_left, scale_right)),
        out_shape=(
            jax.ShapeDtypeStruct(out_grad.shape, bf16),
            jax.ShapeDtypeStruct(hidden.shape, bf16),
            jax.ShapeDtypeStruct((experts, rank, own), f32),
            jax.ShapeDtypeStruct((experts, rank, columns), f32),
        ),
        in_specs=[
            vmem, pl.BlockSpec(memory_space=pl.ANY), vmem, vmem, vmem, vmem, vmem, vmem, vmem,
            pl.BlockSpec(memory_space=pltpu.SMEM),
        ],
        out_specs=(vmem,) * 4,
        scratch_shapes=[
            pltpu.VMEM((experts, rows_all, hidden_width), bf16),
            pltpu.VMEM((experts, columns, hidden_width), bf16),
            pltpu.VMEM((outer_size * block, tokens), f32),
            pltpu.VMEM((outer_size, block, columns), bf16),
            pltpu.VMEM((outer_size, block, columns), bf16),
            pltpu.VMEM((experts, rows_all, columns), bf16),
            pltpu.VMEM((experts, rows_all, hidden_width), bf16),
            pltpu.VMEM((experts, yn - 1, 2, block, hidden_width), bf16),
            pltpu.VMEM((experts, block, hidden_width), bf16),
            pltpu.VMEM((outer_size, block, columns), bf16),
            pltpu.VMEM((outer_size, block, columns), bf16),
        ]
        + [
            pltpu.VMEM((chip_size, piece, lanes), f32),
            pltpu.VMEM((chip_size, piece, lanes), f32),
            pltpu.VMEM((piece, lanes), f32),
            pltpu.VMEM((chip_size, piece, lanes), f32),
        ]
        * 2
        + [
            pltpu.VMEM((experts, rank, columns), f32),
            pltpu.VMEM((experts, rank, own), f32),
            pltpu.VMEM((rank, pay_width), bf16),
            pltpu.VMEM((zn, rank, pay_width), bf16),
            pltpu.VMEM((3, rank, pay_width), bf16),
            pltpu.VMEM((4, rank, pay_width), bf16),
            dma,
            dma((experts, yn - 1, 2)),
            dma((experts, yn - 1, 2)),
            dma((experts,)),
            dma((experts,)),
            dma((experts, yn - 1, 2)),
            dma((experts, yn - 1, 2)),
            dma((experts,)),
            dma((experts,)),
            dma((8,)),
            dma((8,)),
        ],
        compiler_params=pltpu.CompilerParams(
            collective_id=0, has_side_effects=True, vmem_limit_bytes=48 * 2**20
        ),
        name="layer",
    )(
        hidden,
        jnp.swapaxes(down_weight, 1, 2),
        out_grad,
        routes.T,
        gates.T,
        omega.T,
        psi.T,
        jnp.swapaxes(left_old, 1, 2),
        jnp.swapaxes(right_old, 1, 2),
        moves,
    )
    return (mixed, hidden_grad, jnp.swapaxes(left_moved, 1, 2), jnp.swapaxes(right_moved, 1, 2))


def solution(mesh):
    in_specs = (
        P("outer", "chip", None),
        P("outer", None, "chip"),
        P("outer", "chip"),
        P("outer", None),
        P("outer", None),
        P("chip", None),
        P(),
        P("outer", "chip", None),
        P("outer", "chip", None),
        P(),
    )
    out_specs = (
        P("outer", "chip"),
        P("outer", "chip", None),
        P("outer", "chip", None),
        P("outer", "chip", None),
    )
    return jax.shard_map(
        on_device, mesh=mesh, in_specs=in_specs, out_specs=out_specs, check_vma=False
    )
```

```python
import functools
import math

import jax
import jax.numpy as jnp
from jax import lax
from jax.experimental import pallas as pl
from jax.experimental.pallas import tpu as pltpu
from jax.sharding import PartitionSpec as P

MESH = pl.DeviceIdType.MESH


def dot(a, b, a_dim, b_dim):
    return lax.dot_general(
        a, b, (((a_dim,), (b_dim,)), ((), ())), preferred_element_type=jnp.float32
    )


def halves(a):
    high = a.astype(jnp.bfloat16)
    return high, (a - high.astype(jnp.float32)).astype(jnp.bfloat16)


def dot_halves(a, b, b_dim):
    high, low = halves(a)
    both = dot(jnp.concatenate([high, low], axis=0), b, 1, b_dim)
    return both[: a.shape[0]] + both[a.shape[0] :]


def kernel(
    sizes,
    hid_in, wt_in, og_in, routes_in, gates_in, om_in, ps_in, left_in, right_in, moves_in,
    mixed, hidden_grad, left_out, right_out,
    hid, wv, og, routes, gates, om, ps, left_old, right_old, moves,
    full, assign, ob, gb, grad, part, rs_in, rx_in, x_in, eo, rb,
    pm, tp, uw, ur, us, ui, uo, ua, rn, ln, tzr, tzl, sel, t2,
    in_sem, tz_s, tz_r, ag_s, ag_r, agx_s, agx_r, rs_s, rs_r, rx_s, rx_r, one_s, one_r,
):
    outer_size, chip_size, zn, yn, scale_left, scale_right = sizes
    o, c = lax.axis_index("outer"), lax.axis_index("chip")
    z, sub = o // 4, o % 4
    y, xl = c // 2, c % 2
    experts, block, hidden_width = hid.shape
    columns = og.shape[1]
    rank = om.shape[0]
    rows_all = full.shape[1]
    own = left_old.shape[2]
    far = yn // 2

    barrier = pltpu.get_barrier_semaphore()

    @pl.loop(1, outer_size)
    def _(i):
        pl.semaphore_signal(barrier, inc=1, device_id=((o + i) % outer_size, c), device_id_type=MESH)

    @pl.loop(1, chip_size)
    def _(i):
        pl.semaphore_signal(barrier, inc=1, device_id=(o, (c + i) % chip_size), device_id_type=MESH)

    come_in = [
        pltpu.make_async_copy(src, dst, in_sem.at[n])
        for n, (src, dst) in enumerate(
            [
                (hid_in, hid), (routes_in, routes), (gates_in, gates), (og_in, og), (om_in, om), (ps_in, ps),
                (wt_in, wv), (left_in, left_old), (right_in, right_old), (moves_in, moves),
            ]
        )
    ]
    for copy in come_in:
        copy.start()
    def rows(chip):
        return pl.ds(pl.multiple_of(chip * block, block), block)

    come_in[0].wait()
    pl.semaphore_wait(barrier, outer_size + chip_size - 2)

    def remote(src, dst, send, recv, device):
        return pltpu.make_async_remote_copy(
            src_ref=src, dst_ref=dst, send_sem=send, recv_sem=recv, device_id=device, device_id_type=MESH
        )

    x_partner = (o, 2 * y + 1 - xl)

    def around(steps):
        return (y + steps + 2 * yn) % yn

    EXPERT = (1, 0, 0)
    FAR_WAY = (1, -1, 1)
    WAYS = (1, -1)

    def reach(d, t):
        return far if d == FAR_WAY[t] else far - 1

    def chip_of(y_at, t):
        return 2 * y_at + (1 - xl if t == 2 else xl)

    def ag_copy(d, s, t):
        source = rows(chip_of(around(-d * s), t))
        k = EXPERT[t]
        src = hid.at[k] if s == 0 and t < 2 else full.at[k, source]
        n = WAYS.index(d)
        return remote(
            src, full.at[k, source], ag_s.at[n, s, t], ag_r.at[n, s, t], (o, 2 * around(d) + xl)
        )

    def ag_x(n, k, y_at):
        source = rows(2 * y_at + xl)
        src = hid.at[k] if n < 2 else full.at[k, source]
        return remote(src, full.at[k, source], agx_s.at[n], agx_r.at[n], x_partner)

    def ag_x_of(d, s):
        return ag_x(2 + WAYS.index(d) * far + s, 1, around(-d * (s + 1)))

    def ag_step(s):
        for t in range(3):
            for d in WAYS:
                if s < reach(d, t):
                    ag_copy(d, s, t).wait_recv()
                    if s + 1 < reach(d, t):
                        ag_copy(d, s + 1, t).start()
                    if t == 0:
                        ag_x_of(d, s).start()

    ag_x(0, 0, y).start()
    for t in range(2):
        for d in WAYS:
            if reach(d, t):
                ag_copy(d, 0, t).start()
    ag_x(1, 1, y).start()

    def spread(src_of, dst, number, axis_size, device_of):
        @pl.loop(1, axis_size)
        def _(i):
            remote(src_of(i), dst, one_s.at[number], one_r.at[number], device_of(i)).start()

    def arrived(buf, count, number):
        ref = buf.at[pl.ds(0, count)]
        pltpu.make_async_copy(ref, ref, one_r.at[number]).wait()

    def sent(buf, count, number):
        ref = buf.at[pl.ds(0, count)]
        pltpu.make_async_copy(ref, ref, one_s.at[number]).wait()

    def other_group(i):
        return (o + i) % outer_size

    def other_chip(i):
        return (c + i) % chip_size

    for copy in come_in[1:5]:
        copy.wait()
    routes_now, gates_now = routes[...], gates[...]
    tokens = routes_now.shape[1]
    place = lax.broadcasted_iota(jnp.int32, assign.shape, 0)
    expert = lax.shift_right_logical(place, 3)
    slot = (place & 7).astype(jnp.float32)
    picked = jnp.zeros(assign.shape, jnp.float32)
    weight = jnp.zeros(assign.shape, jnp.float32)
    for p in range(routes_now.shape[0]):
        hit = routes_now[p : p + 1, :] == expert
        picked = picked + jnp.where(hit, 1.0, 0.0)
        weight = weight + jnp.where(hit, gates_now[p : p + 1, :], 0.0)
    earlier = lax.broadcasted_iota(jnp.int32, (tokens, tokens), 0) < lax.broadcasted_iota(
        jnp.int32, (tokens, tokens), 1
    )
    ranks = dot(picked.astype(jnp.bfloat16), jnp.where(earlier, 1.0, 0.0).astype(jnp.bfloat16), 1, 0)
    weight = jnp.where(ranks == slot, weight, 0.0)
    assign[...] = weight
    high, low = halves(weight)
    og_now = og[...]
    outgoing = dot(high, og_now, 1, 0) + dot(low, og_now, 1, 0)
    ob[...] = outgoing.astype(jnp.bfloat16).reshape(ob.shape)
    gb[o] = ob[o]

    spread(lambda i: ob.at[other_group(i)], gb.at[o], 0, outer_size, lambda i: (other_group(i), c))

    token_cols = dot_halves(om[...], og_now, 1)
    fold = rank // 2
    tp[c] = jnp.concatenate([token_cols[:fold], token_cols[fold:]], axis=1).astype(jnp.bfloat16)
    spread(lambda i: tp.at[c], tp.at[c], 2, chip_size, lambda i: (o, other_chip(i)))

    for copy in come_in[5:]:
        copy.wait()
    for k in range(experts):
        full[k, rows(c), :] = hid[k]
    psi_high, psi_low = halves(ps[...])
    pm[c] = jnp.concatenate([dot(hid[k], psi_high, 1, 1) + dot(hid[k], psi_low, 1, 1) for k in range(experts)], axis=1)
    spread(lambda i: pm.at[c], pm.at[c], 3, chip_size, lambda i: (o, other_chip(i)))

    ag_x(0, 0, y).wait_recv()
    for d in WAYS:
        if reach(d, 2):
            ag_copy(d, 0, 2).start()
    for s in range(far - 1):
        ag_step(s)

    arrived(tp, chip_size - 1, 2)
    token_cols = jnp.sum(tp[...].astype(jnp.float32), axis=0)
    token_cols = jnp.concatenate([token_cols[:, :tokens], token_cols[:, tokens:]], axis=0)
    uw[...] = dot_halves(assign[...], token_cols.astype(jnp.bfloat16), 1).astype(jnp.bfloat16).reshape(uw.shape)
    ur[o] = uw[o]
    spread(lambda i: uw.at[other_group(i)], ur.at[o], 4, outer_size, lambda i: (other_group(i), c))

    arrived(gb, outer_size - 1, 0)
    eight = block // experts
    come = gb[...].astype(jnp.float32)
    for k in range(experts):
        grad[k] = come[:, k * eight : (k + 1) * eight, :].reshape(rows_all, columns).astype(jnp.bfloat16)

    lanes = us.shape[2]
    lane_cuts = rows_all // lanes
    piece = us.shape[1]

    def sum_send(parts, send, into, number):
        both = jnp.concatenate(parts, axis=0)
        for p in range(chip_size):
            at, cut = p // lane_cuts, p % lane_cuts
            send[p] = both[at * piece : (at + 1) * piece, cut * lanes : (cut + 1) * lanes]
        into[c] = send[c]
        spread(lambda i: send.at[other_chip(i)], into.at[c], number, chip_size, lambda i: (o, other_chip(i)))

    def sum_share(into, own_sum, full_sum, number):
        arrived(into, chip_size - 1, number)
        own_sum[...] = jnp.sum(into[...], axis=0)
        full_sum[c] = own_sum[...]
        spread(lambda i: own_sum, full_sum.at[c], 8, chip_size, lambda i: (o, other_chip(i)))

    def sum_take(full_sum):
        arrived(full_sum, chip_size - 1, 8)
        lines = []
        for at in range(chip_size // lane_cuts):
            lines.append(
                jnp.concatenate([full_sum[at * lane_cuts + cut] for cut in range(lane_cuts)], axis=1)
            )
        return jnp.concatenate(lines, axis=0)

    sums = []
    arrived(pm, chip_size - 1, 3)
    row_psi = pm[...].reshape(rows_all, experts * rank)
    psi_high, psi_low = halves(row_psi)
    for k in range(experts):
        both = jnp.concatenate([psi_high[:, k * rank : (k + 1) * rank], psi_low[:, k * rank : (k + 1) * rank]], axis=1)
        both = dot(both, grad[k], 0, 0)
        sums.append(dot_halves(both[:rank] + both[rank:], grad[k], 1))
    sum_send(sums, us, ui, 1)

    tile = min(512, hidden_width)

    def partial_of(k):
        @pl.loop(0, hidden_width // tile)
        def _(n):
            cut = pl.ds(pl.multiple_of(n * tile, tile), tile)
            part[k, :, cut] = dot(grad[k], wv[k, :, cut], 1, 0).astype(jnp.bfloat16)

    def rs_rows(d, m, t):
        return rows(chip_of(around(d * m), t))

    def rs_copy(d, m, t):
        n = WAYS.index(d)
        return remote(
            part.at[EXPERT[t], rs_rows(d, m, t)],
            rs_in.at[n, m - 1, t],
            rs_s.at[n, m - 1, t],
            rs_r.at[n, m - 1, t],
            (o, 2 * around(d) + xl),
        )

    def rx_copy(r):
        src = part.at[1, rows(2 * around(r) + 1 - xl)]
        return remote(src, rx_in.at[r], rx_s.at[r], rx_r.at[r], x_partner)

    def rx_add(r):
        rx_copy(r).wait_recv()
        at = rows(2 * around(r) + xl)
        part[1, at, :] = (part[1, at, :].astype(jnp.float32) + rx_in[r].astype(jnp.float32)).astype(jnp.bfloat16)

    def rs_start(d, t):
        if t == 0:
            rx_add(d * reach(d, t) % yn)
        rs_copy(d, reach(d, t), t).start()

    def rs_first(t):
        for d in WAYS:
            if reach(d, t):
                rs_start(d, t)

    def rs_relay(d, m, t):
        if t == 0:
            rx_add(d * m % yn)
        rs_copy(d, m + 1, t).wait_recv()
        at = rs_rows(d, m, t)
        total = part[EXPERT[t], at, :].astype(jnp.float32) + rs_in[WAYS.index(d), m, t].astype(jnp.float32)
        part[EXPERT[t], at, :] = total.astype(jnp.bfloat16)
        rs_copy(d, m, t).start()

    todo = []
    for m in range(far - 1, 0, -1):
        for t in (1, 2, 0):
            if t == 0 and m == far - 1:
                todo += [functools.partial(rs_start, d, 0) for d in WAYS if reach(d, 0)]
            for d in WAYS:
                if m < reach(d, t):
                    todo.append(functools.partial(rs_relay, d, m, t))
    if far == 1:
        todo += [functools.partial(rs_start, d, 0) for d in WAYS if reach(d, 0)]

    def rs_do(count):
        for _ in range(min(count, len(todo))):
            todo.pop(0)()

    def rs_total(t):
        total = part[EXPERT[t], rs_rows(1, 0, t), :].astype(jnp.float32)
        for d in WAYS:
            if reach(d, t):
                rs_copy(d, 1, t).wait_recv()
                total = total + rs_in[WAYS.index(d), 0, t].astype(jnp.float32)
        return total

    def last_x():
        return remote(part.at[0, rs_rows(1, 0, 2)], x_in, rx_s.at[yn], rx_r.at[yn], x_partner)

    partial_of(0)
    rs_first(1)
    rs_first(2)
    ag_step(far - 1)
    partial_of(1)
    order = sorted(range(yn), key=lambda r: -min(r, yn - r))
    for r in order:
        rx_copy(r).start()
    arrived(ur, outer_size - 1, 4)
    cols = ur[...].astype(jnp.float32)
    ag_x(1, 1, y).wait_recv()
    for d in WAYS:
        for s in range(reach(d, 0)):
            ag_x_of(d, s).wait_recv()

    def tz_reach(d):
        return zn // 2 if d == -1 else zn // 2 - 1

    def tz_copy(d, s):
        at = (z - d * s + 2 * zn) % zn
        n = WAYS.index(d)
        return remote(
            tzr.at[at], tzr.at[at], tz_s.at[n, s], tz_r.at[n, s], (((z + d + zn) % zn) * 4 + sub, c)
        )

    def tz_step(s):
        for d in WAYS:
            if s < tz_reach(d):
                tz_copy(d, s).wait_recv()
                if s + 1 < tz_reach(d):
                    tz_copy(d, s + 1).start()

    for k in range(experts):
        row_cols = cols[:, k * eight : (k + 1) * eight, :].reshape(rows_all, rank).astype(jnp.bfloat16)
        sketch = dot(row_cols, full[k], 0, 0)
        row_width = dot_halves(sketch, full[k], 1)
        rn[k] = 0.5 * right_old[k] + 0.5 * scale_right * dot_halves(row_width, grad[k], 0)
        tzr[z, :, k * columns : (k + 1) * columns] = rn[k].astype(jnp.bfloat16)
    for d in WAYS:
        if tz_reach(d):
            tz_copy(d, 0).start()
    sum_share(ui, uo, ua, 1)

    outputs = []
    for k in range(experts):
        outputs.append(dot(full[k], wv[k], 1, 1).reshape(outer_size, eight, columns))
        rs_do(2)
    eo[...] = jnp.concatenate(outputs, axis=1).astype(jnp.bfloat16)
    rb[o] = eo[o]
    spread(lambda i: eo.at[other_group(i)], rb.at[o], 5, outer_size, lambda i: (other_group(i), c))
    rs_do(1)
    tz_step(0)
    rs_do(4)
    if zn > 2:
        tz_step(1)

    sums = sum_take(ua)
    mine = pl.ds(pl.multiple_of(c * own, own), own)
    for k in range(experts):
        row_left = sums[k * rank : (k + 1) * rank]
        ln[k] = 0.5 * left_old[k] + 0.5 * scale_left * dot_halves(row_left, full[k, :, mine], 0)
        tzl[z, :, k * own : (k + 1) * own] = ln[k].astype(jnp.bfloat16)
    spread(lambda i: tzl.at[z], tzl.at[z], 6, zn, lambda i: (((z + i) % zn) * 4 + sub, c))

    def source_of(group):
        source = group
        for m in range(moves.shape[1]):
            a, b = moves[0, m], moves[1, m]
            source = jnp.where(group == a, b, jnp.where(group == b, a, source))
        return source

    rs_do(2)
    rs_do(2)
    for s in range(2, zn // 2):
        tz_step(s)
        rs_do(4)

    right_width = experts * columns
    arrived(tzl, zn - 1, 6)
    for i in range(1, 4):
        at = lax.shift_right_logical(source_of(z * 4 + (sub + i) % 4), 2)
        sel[i - 1, :, :right_width] = tzr[at]
        sel[i - 1, :, right_width:] = tzl[at]
        remote(
            sel.at[i - 1], t2.at[sub], one_s.at[7], one_r.at[7], (z * 4 + (sub + i) % 4, c)
        ).start()
    mine_from = source_of(o)
    at = lax.shift_right_logical(mine_from, 2)
    t2[sub, :, :right_width] = tzr[at]
    t2[sub, :, right_width:] = tzl[at]

    rs_do(len(todo))
    part[0, rs_rows(1, 0, 2), :] = rs_total(2).astype(jnp.bfloat16)
    last_x().start()
    rx_add(0)
    hidden_grad[1] = rs_total(0).astype(jnp.bfloat16)
    total = rs_total(1)

    arrived(rb, outer_size - 1, 5)
    back = rb[...].reshape(outer_size * block, columns)
    high, low = halves(assign[...])
    mixed[...] = (dot(high, back, 0, 0) + dot(low, back, 0, 0)).astype(jnp.bfloat16)

    last_x().wait_recv()
    hidden_grad[0] = (total + x_in[...].astype(jnp.float32)).astype(jnp.bfloat16)

    stays = mine_from == o
    arrived(t2, 3, 7)
    came = t2[mine_from & 3].astype(jnp.float32)
    for k in range(experts):
        right_out[k] = jnp.where(stays, rn[k], came[:, k * columns : (k + 1) * columns])
        at = right_width + k * own
        left_out[k] = jnp.where(stays, ln[k], came[:, at : at + own])

    ag_x(0, 0, y).wait_send()
    ag_x(1, 1, y).wait_send()
    for d in WAYS:
        for s in range(reach(d, 0)):
            ag_x_of(d, s).wait_send()
        for t in range(3):
            for s in range(reach(d, t)):
                ag_copy(d, s, t).wait_send()
                rs_copy(d, s + 1, t).wait_send()
    for r in range(yn):
        rx_copy(r).wait_send()
    last_x().wait_send()
    sent(ob, outer_size - 1, 0)
    sent(us, chip_size - 1, 1)
    sent(ua, chip_size - 1, 8)
    sent(tp, chip_size - 1, 2)
    sent(pm, chip_size - 1, 3)
    sent(uw, outer_size - 1, 4)
    sent(eo, outer_size - 1, 5)
    sent(tzl, zn - 1, 6)
    sent(sel, 3, 7)
    for d in WAYS:
        for s in range(tz_reach(d)):
            tz_copy(d, s).wait_send()


def on_device(hidden, down_weight, out_grad, routes, gates, omega, psi, left_old, right_old, moves):
    outer_size = lax.axis_size("outer")
    chip_size = lax.axis_size("chip")
    experts, hidden_width, columns = down_weight.shape
    model_width = columns * chip_size
    block = hidden.shape[1]
    rows_all = block * chip_size
    own = left_old.shape[1]
    rank = omega.shape[1]
    tokens = routes.shape[0]
    zn, yn = outer_size // 4, chip_size // 2
    scale_right = 10.0 / (rows_all * (hidden_width / math.sqrt(model_width) + math.sqrt(hidden_width)))
    scale_left = 10.0 / (rows_all * (model_width / math.sqrt(hidden_width) + math.sqrt(model_width)))
    far = yn // 2
    lanes = min(rows_all, 128)
    piece = experts * rank * (rows_all // lanes) // chip_size
    pay_width = experts * (columns + own)
    bf16, f32 = jnp.bfloat16, jnp.float32
    dma = pltpu.SemaphoreType.DMA
    vmem = pl.BlockSpec(memory_space=pltpu.VMEM)
    operands = (
        hidden,
        jnp.swapaxes(down_weight, 1, 2),
        out_grad,
        routes.T,
        gates.T,
        omega.T,
        psi.T,
        jnp.swapaxes(left_old, 1, 2),
        jnp.swapaxes(right_old, 1, 2),
        moves.T,
    )
    mixed, hidden_grad, left_moved, right_moved = pl.pallas_call(
        functools.partial(kernel, (outer_size, chip_size, zn, yn, scale_left, scale_right)),
        out_shape=(
            jax.ShapeDtypeStruct(out_grad.shape, bf16),
            jax.ShapeDtypeStruct(hidden.shape, bf16),
            jax.ShapeDtypeStruct((experts, rank, own), f32),
            jax.ShapeDtypeStruct((experts, rank, columns), f32),
        ),
        in_specs=[pl.BlockSpec(memory_space=pl.ANY)] * len(operands),
        out_specs=(vmem,) * 4,
        scratch_shapes=[pltpu.VMEM(a.shape, a.dtype) for a in operands[:-1]]
        + [
            pltpu.SMEM(operands[-1].shape, jnp.int32),
            pltpu.VMEM((experts, rows_all, hidden_width), bf16),
            pltpu.VMEM((outer_size * block, tokens), f32),
            pltpu.VMEM((outer_size, block, columns), bf16),
            pltpu.VMEM((outer_size, block, columns), bf16),
            pltpu.VMEM((experts, rows_all, columns), bf16),
            pltpu.VMEM((experts, rows_all, hidden_width), bf16),
            pltpu.VMEM((2, far, 3, block, hidden_width), bf16),
            pltpu.VMEM((yn, block, hidden_width), bf16),
            pltpu.VMEM((block, hidden_width), bf16),
            pltpu.VMEM((outer_size, block, columns), bf16),
            pltpu.VMEM((outer_size, block, columns), bf16),
            pltpu.VMEM((chip_size, block, experts * rank), f32),
            pltpu.VMEM((chip_size, rank // 2, 2 * tokens), bf16),
            pltpu.VMEM((outer_size, block, rank), bf16),
            pltpu.VMEM((outer_size, block, rank), bf16),
            pltpu.VMEM((chip_size, piece, lanes), f32),
            pltpu.VMEM((chip_size, piece, lanes), f32),
            pltpu.VMEM((piece, lanes), f32),
            pltpu.VMEM((chip_size, piece, lanes), f32),
            pltpu.VMEM((experts, rank, columns), f32),
            pltpu.VMEM((experts, rank, own), f32),
            pltpu.VMEM((zn, rank, experts * columns), bf16),
            pltpu.VMEM((zn, rank, experts * own), bf16),
            pltpu.VMEM((3, rank, pay_width), bf16),
            pltpu.VMEM((4, rank, pay_width), bf16),
            dma((len(operands),)),
            dma((2, zn // 2)),
            dma((2, zn // 2)),
            dma((2, far, 3)),
            dma((2, far, 3)),
            dma((2 + 2 * far,)),
            dma((2 + 2 * far,)),
            dma((2, far, 3)),
            dma((2, far, 3)),
            dma((yn + 1,)),
            dma((yn + 1,)),
            dma((9,)),
            dma((9,)),
        ],
        compiler_params=pltpu.CompilerParams(
            collective_id=0, has_side_effects=True, vmem_limit_bytes=64 * 2**20
        ),
        name="layer",
    )(*operands)
    return (mixed, hidden_grad, jnp.swapaxes(left_moved, 1, 2), jnp.swapaxes(right_moved, 1, 2))


def solution(mesh):
    in_specs = (
        P("outer", "chip", None),
        P("outer", None, "chip"),
        P("outer", "chip"),
        P("outer", None),
        P("outer", None),
        P("chip", None),
        P(),
        P("outer", "chip", None),
        P("outer", "chip", None),
        P(),
    )
    out_specs = (
        P("outer", "chip"),
        P("outer", "chip", None),
        P("outer", "chip", None),
        P("outer", "chip", None),
    )
    return jax.shard_map(
        on_device, mesh=mesh, in_specs=in_specs, out_specs=out_specs, check_vma=False
    )
```

```python
import functools
import math

import jax
import jax.numpy as jnp
from jax import lax
from jax.experimental import pallas as pl
from jax.experimental.pallas import tpu as pltpu
from jax.sharding import PartitionSpec as P

MESH = pl.DeviceIdType.MESH


def dot(a, b, a_dim, b_dim):
    return lax.dot_general(
        a, b, (((a_dim,), (b_dim,)), ((), ())), preferred_element_type=jnp.float32
    )


def halves(a):
    high = a.astype(jnp.bfloat16)
    return high, (a - high.astype(jnp.float32)).astype(jnp.bfloat16)


def dot_halves(a, b, b_dim):
    high, low = halves(a)
    both = dot(jnp.concatenate([high, low], axis=0), b, 1, b_dim)
    return both[: a.shape[0]] + both[a.shape[0] :]


def kernel(
    sizes,
    hid_in, wt_in, og_in, routes_in, gates_in, om_in, ps_in, left_in, right_in, moves_in,
    mixed_to, hidden_grad_to, left_to, right_to,
    mixed, hidden_grad, left_out, right_out,
    hid, wv, og, routes, gates, om, ps, left_old, right_old, moves,
    full, assign, ob, gb, grad, part, rs_in, rx_in, x_in, eo, rb,
    pm, tp, uw, ur, us, ui, uo, ua, rn, ln, tzr, tzl, sel, t2,
    in_sem, out_sem, ag_s, ag_r, agx_s, agx_r, rs_s, rs_r, rx_s, rx_r, one_s, one_r,
):
    outer_size, chip_size, zn, yn, scale_left, scale_right = sizes
    o, c = lax.axis_index("outer"), lax.axis_index("chip")
    z, sub = o // 4, o % 4
    y, xl = c // 2, c % 2
    experts, block, hidden_width = hid.shape
    columns = og.shape[1]
    rank = om.shape[0]
    rows_all = full.shape[1]
    own = left_old.shape[2]
    far = yn // 2

    barrier = pltpu.get_barrier_semaphore()

    @pl.loop(1, outer_size)
    def _(i):
        pl.semaphore_signal(barrier, inc=1, device_id=((o + i) % outer_size, c), device_id_type=MESH)

    @pl.loop(1, chip_size)
    def _(i):
        pl.semaphore_signal(barrier, inc=1, device_id=(o, (c + i) % chip_size), device_id_type=MESH)

    come_in = [
        pltpu.make_async_copy(src, dst, in_sem.at[n])
        for n, (src, dst) in enumerate(
            [
                (hid_in, hid), (routes_in, routes), (gates_in, gates), (og_in, og), (om_in, om), (ps_in, ps),
                (wt_in, wv), (left_in, left_old), (right_in, right_old), (moves_in, moves),
            ]
        )
    ]
    for copy in come_in:
        copy.start()
    go_out = [
        pltpu.make_async_copy(src, dst, out_sem.at[n])
        for n, (src, dst) in enumerate(
            [(mixed, mixed_to), (hidden_grad, hidden_grad_to), (left_out, left_to), (right_out, right_to)]
        )
    ]
    def rows(chip):
        return pl.ds(pl.multiple_of(chip * block, block), block)

    come_in[0].wait()
    pl.semaphore_wait(barrier, outer_size + chip_size - 2)

    def remote(src, dst, send, recv, device):
        return pltpu.make_async_remote_copy(
            src_ref=src, dst_ref=dst, send_sem=send, recv_sem=recv, device_id=device, device_id_type=MESH
        )

    x_partner = (o, 2 * y + 1 - xl)

    def around(steps):
        return (y + steps + 2 * yn) % yn

    EXPERT = (1, 0, 0)
    FAR_WAY = (1, -1, 1)
    WAYS = (1, -1)

    def reach(d, t):
        return far if d == FAR_WAY[t] else far - 1

    def chip_of(y_at, t):
        return 2 * y_at + (1 - xl if t == 2 else xl)

    def ag_copy(d, s, t):
        source = rows(chip_of(around(-d * s), t))
        k = EXPERT[t]
        src = hid.at[k] if s == 0 and t < 2 else full.at[k, source]
        n = WAYS.index(d)
        return remote(
            src, full.at[k, source], ag_s.at[n, s, t], ag_r.at[n, s, t], (o, 2 * around(d) + xl)
        )

    def ag_x(n, k, y_at):
        source = rows(2 * y_at + xl)
        src = hid.at[k] if n < 2 else full.at[k, source]
        return remote(src, full.at[k, source], agx_s.at[n], agx_r.at[n], x_partner)

    def ag_x_of(d, s):
        return ag_x(2 + WAYS.index(d) * far + s, 1, around(-d * (s + 1)))

    def ag_step(s):
        for t in range(3):
            for d in WAYS:
                if s < reach(d, t):
                    ag_copy(d, s, t).wait_recv()
                    if s + 1 < reach(d, t):
                        ag_copy(d, s + 1, t).start()
                    if t == 0:
                        ag_x_of(d, s).start()

    ag_x(0, 0, y).start()
    for t in range(2):
        for d in WAYS:
            if reach(d, t):
                ag_copy(d, 0, t).start()
    ag_x(1, 1, y).start()

    def spread(src_of, dst, number, axis_size, device_of):
        @pl.loop(1, axis_size)
        def _(i):
            remote(src_of(i), dst, one_s.at[number], one_r.at[number], device_of(i)).start()

    def arrived(buf, count, number):
        ref = buf.at[pl.ds(0, count)]
        pltpu.make_async_copy(ref, ref, one_r.at[number]).wait()

    def sent(buf, count, number):
        ref = buf.at[pl.ds(0, count)]
        pltpu.make_async_copy(ref, ref, one_s.at[number]).wait()

    def other_group(i):
        return (o + i) % outer_size

    def other_chip(i):
        return (c + i) % chip_size

    for copy in come_in[1:5]:
        copy.wait()
    routes_now, gates_now = routes[...], gates[...]
    tokens = routes_now.shape[1]
    place = lax.broadcasted_iota(jnp.int32, assign.shape, 0)
    expert = lax.shift_right_logical(place, 3)
    slot = (place & 7).astype(jnp.float32)
    picked = jnp.zeros(assign.shape, jnp.float32)
    weight = jnp.zeros(assign.shape, jnp.float32)
    for p in range(routes_now.shape[0]):
        hit = routes_now[p : p + 1, :] == expert
        picked = picked + jnp.where(hit, 1.0, 0.0)
        weight = weight + jnp.where(hit, gates_now[p : p + 1, :], 0.0)
    earlier = lax.broadcasted_iota(jnp.int32, (tokens, tokens), 0) < lax.broadcasted_iota(
        jnp.int32, (tokens, tokens), 1
    )
    ranks = dot(picked.astype(jnp.bfloat16), jnp.where(earlier, 1.0, 0.0).astype(jnp.bfloat16), 1, 0)
    weight = jnp.where(ranks == slot, weight, 0.0)
    assign[...] = weight
    high, low = halves(weight)
    og_now = og[...]
    outgoing = dot(high, og_now, 1, 0) + dot(low, og_now, 1, 0)
    ob[...] = outgoing.astype(jnp.bfloat16).reshape(ob.shape)
    gb[o] = ob[o]

    spread(lambda i: ob.at[other_group(i)], gb.at[o], 0, outer_size, lambda i: (other_group(i), c))

    token_cols = dot_halves(om[...], og_now, 1)
    fold = rank // 2
    tp[c] = jnp.concatenate([token_cols[:fold], token_cols[fold:]], axis=1).astype(jnp.bfloat16)
    spread(lambda i: tp.at[c], tp.at[c], 2, chip_size, lambda i: (o, other_chip(i)))

    for copy in come_in[5:]:
        copy.wait()
    for k in range(experts):
        full[k, rows(c), :] = hid[k]
    psi_high, psi_low = halves(ps[...])
    pm[c] = jnp.concatenate([dot(hid[k], psi_high, 1, 1) + dot(hid[k], psi_low, 1, 1) for k in range(experts)], axis=1)
    spread(lambda i: pm.at[c], pm.at[c], 3, chip_size, lambda i: (o, other_chip(i)))

    ag_x(0, 0, y).wait_recv()
    for d in WAYS:
        if reach(d, 2):
            ag_copy(d, 0, 2).start()
    for s in range(far - 1):
        ag_step(s)

    arrived(tp, chip_size - 1, 2)
    token_cols = jnp.sum(tp[...].astype(jnp.float32), axis=0)
    token_cols = jnp.concatenate([token_cols[:, :tokens], token_cols[:, tokens:]], axis=0)
    uw[...] = dot_halves(assign[...], token_cols.astype(jnp.bfloat16), 1).astype(jnp.bfloat16).reshape(uw.shape)
    ur[o] = uw[o]
    spread(lambda i: uw.at[other_group(i)], ur.at[o], 4, outer_size, lambda i: (other_group(i), c))

    arrived(gb, outer_size - 1, 0)
    eight = block // experts
    come = gb[...].astype(jnp.float32)
    for k in range(experts):
        grad[k] = come[:, k * eight : (k + 1) * eight, :].reshape(rows_all, columns).astype(jnp.bfloat16)

    lanes = us.shape[2]
    lane_cuts = rows_all // lanes
    piece = us.shape[1]

    def sum_send(parts, send, into, number):
        both = jnp.concatenate(parts, axis=0)
        for p in range(chip_size):
            at, cut = p // lane_cuts, p % lane_cuts
            send[p] = both[at * piece : (at + 1) * piece, cut * lanes : (cut + 1) * lanes]
        into[c] = send[c]
        spread(lambda i: send.at[other_chip(i)], into.at[c], number, chip_size, lambda i: (o, other_chip(i)))

    def sum_share(into, own_sum, full_sum, number):
        arrived(into, chip_size - 1, number)
        own_sum[...] = jnp.sum(into[...], axis=0)
        full_sum[c] = own_sum[...]
        spread(lambda i: own_sum, full_sum.at[c], 8, chip_size, lambda i: (o, other_chip(i)))

    def sum_take(full_sum):
        arrived(full_sum, chip_size - 1, 8)
        lines = []
        for at in range(chip_size // lane_cuts):
            lines.append(
                jnp.concatenate([full_sum[at * lane_cuts + cut] for cut in range(lane_cuts)], axis=1)
            )
        return jnp.concatenate(lines, axis=0)

    sums = []
    arrived(pm, chip_size - 1, 3)
    row_psi = pm[...].reshape(rows_all, experts * rank)
    psi_high, psi_low = halves(row_psi)
    for k in range(experts):
        both = jnp.concatenate([psi_high[:, k * rank : (k + 1) * rank], psi_low[:, k * rank : (k + 1) * rank]], axis=1)
        both = dot(both, grad[k], 0, 0)
        sums.append(dot_halves(both[:rank] + both[rank:], grad[k], 1))
    sum_send(sums, us, ui, 1)

    tile = min(512, hidden_width)

    def partial_of(k):
        @pl.loop(0, hidden_width // tile)
        def _(n):
            cut = pl.ds(pl.multiple_of(n * tile, tile), tile)
            part[k, :, cut] = dot(grad[k], wv[k, :, cut], 1, 0).astype(jnp.bfloat16)

    def rs_rows(d, m, t):
        return rows(chip_of(around(d * m), t))

    def rs_copy(d, m, t):
        n = WAYS.index(d)
        return remote(
            part.at[EXPERT[t], rs_rows(d, m, t)],
            rs_in.at[n, m - 1, t],
            rs_s.at[n, m - 1, t],
            rs_r.at[n, m - 1, t],
            (o, 2 * around(d) + xl),
        )

    def rx_copy(r):
        src = part.at[1, rows(2 * around(r) + 1 - xl)]
        return remote(src, rx_in.at[r], rx_s.at[r], rx_r.at[r], x_partner)

    def rx_add(r):
        rx_copy(r).wait_recv()
        at = rows(2 * around(r) + xl)
        part[1, at, :] = (part[1, at, :].astype(jnp.float32) + rx_in[r].astype(jnp.float32)).astype(jnp.bfloat16)

    def rs_start(d, t):
        if t == 0:
            rx_add(d * reach(d, t) % yn)
        rs_copy(d, reach(d, t), t).start()

    def rs_first(t):
        for d in WAYS:
            if reach(d, t):
                rs_start(d, t)

    def rs_relay(d, m, t):
        if t == 0:
            rx_add(d * m % yn)
        rs_copy(d, m + 1, t).wait_recv()
        at = rs_rows(d, m, t)
        total = part[EXPERT[t], at, :].astype(jnp.float32) + rs_in[WAYS.index(d), m, t].astype(jnp.float32)
        part[EXPERT[t], at, :] = total.astype(jnp.bfloat16)
        rs_copy(d, m, t).start()

    todo = []
    for m in range(far - 1, 0, -1):
        for t in (1, 2, 0):
            if t == 0 and m == far - 1:
                todo += [functools.partial(rs_start, d, 0) for d in WAYS if reach(d, 0)]
            for d in WAYS:
                if m < reach(d, t):
                    todo.append(functools.partial(rs_relay, d, m, t))
    if far == 1:
        todo += [functools.partial(rs_start, d, 0) for d in WAYS if reach(d, 0)]

    def rs_do(count):
        for _ in range(min(count, len(todo))):
            todo.pop(0)()

    def rs_total(t):
        total = part[EXPERT[t], rs_rows(1, 0, t), :].astype(jnp.float32)
        for d in WAYS:
            if reach(d, t):
                rs_copy(d, 1, t).wait_recv()
                total = total + rs_in[WAYS.index(d), 0, t].astype(jnp.float32)
        return total

    def last_x():
        return remote(part.at[0, rs_rows(1, 0, 2)], x_in, rx_s.at[yn], rx_r.at[yn], x_partner)

    partial_of(0)
    rs_first(1)
    rs_first(2)
    ag_step(far - 1)
    partial_of(1)
    order = sorted(range(yn), key=lambda r: -min(r, yn - r))
    for r in order:
        rx_copy(r).start()
    ag_x(1, 1, y).wait_recv()
    for d in WAYS:
        for s in range(reach(d, 0)):
            ag_x_of(d, s).wait_recv()

    outputs = []
    for k in range(experts):
        outputs.append(dot(full[k], wv[k], 1, 1).reshape(outer_size, eight, columns))
    eo[...] = jnp.concatenate(outputs, axis=1).astype(jnp.bfloat16)
    rb[o] = eo[o]
    spread(lambda i: eo.at[other_group(i)], rb.at[o], 5, outer_size, lambda i: (other_group(i), c))
    rs_do(5)
    arrived(ur, outer_size - 1, 4)
    cols = ur[...].astype(jnp.float32)
    for k in range(experts):
        row_cols = cols[:, k * eight : (k + 1) * eight, :].reshape(rows_all, rank).astype(jnp.bfloat16)
        sketch = dot(row_cols, full[k], 0, 0)
        row_width = dot_halves(sketch, full[k], 1)
        rn[k] = 0.5 * right_old[k] + 0.5 * scale_right * dot_halves(row_width, grad[k], 0)
        tzr[z, :, k * columns : (k + 1) * columns] = rn[k].astype(jnp.bfloat16)
    spread(lambda i: tzr.at[z], tzr.at[z], 9, zn, lambda i: (((z + i) % zn) * 4 + sub, c))
    sum_share(ui, uo, ua, 1)
    rs_do(6)

    sums = sum_take(ua)
    mine = pl.ds(pl.multiple_of(c * own, own), own)
    for k in range(experts):
        row_left = sums[k * rank : (k + 1) * rank]
        ln[k] = 0.5 * left_old[k] + 0.5 * scale_left * dot_halves(row_left, full[k, :, mine], 0)
        tzl[z, :, k * own : (k + 1) * own] = ln[k].astype(jnp.bfloat16)
    spread(lambda i: tzl.at[z], tzl.at[z], 6, zn, lambda i: (((z + i) % zn) * 4 + sub, c))

    def source_of(group):
        source = group
        for m in range(moves.shape[1]):
            a, b = moves[0, m], moves[1, m]
            source = jnp.where(group == a, b, jnp.where(group == b, a, source))
        return source

    rs_do(6)
    part[0, rs_rows(1, 0, 2), :] = rs_total(2).astype(jnp.bfloat16)
    last_x().start()
    arrived(tzr, zn - 1, 9)

    right_width = experts * columns
    arrived(tzl, zn - 1, 6)
    for i in range(1, 4):
        at = lax.shift_right_logical(source_of(z * 4 + (sub + i) % 4), 2)
        sel[i - 1, :, :right_width] = tzr[at]
        sel[i - 1, :, right_width:] = tzl[at]
        remote(
            sel.at[i - 1], t2.at[sub], one_s.at[7], one_r.at[7], (z * 4 + (sub + i) % 4, c)
        ).start()
    mine_from = source_of(o)
    at = lax.shift_right_logical(mine_from, 2)
    t2[sub, :, :right_width] = tzr[at]
    t2[sub, :, right_width:] = tzl[at]

    rx_add(0)
    hidden_grad[1] = rs_total(0).astype(jnp.bfloat16)
    total = rs_total(1)

    arrived(rb, outer_size - 1, 5)
    back = rb[...].reshape(outer_size * block, columns)
    high, low = halves(assign[...])
    mixed[...] = (dot(high, back, 0, 0) + dot(low, back, 0, 0)).astype(jnp.bfloat16)

    go_out[0].start()
    last_x().wait_recv()
    hidden_grad[0] = (total + x_in[...].astype(jnp.float32)).astype(jnp.bfloat16)

    go_out[1].start()
    stays = mine_from == o
    arrived(t2, 3, 7)
    came = t2[mine_from & 3].astype(jnp.float32)
    for k in range(experts):
        right_out[k] = jnp.where(stays, rn[k], came[:, k * columns : (k + 1) * columns])
        at = right_width + k * own
        left_out[k] = jnp.where(stays, ln[k], came[:, at : at + own])

    go_out[2].start()
    go_out[3].start()

    ag_x(0, 0, y).wait_send()
    ag_x(1, 1, y).wait_send()
    for d in WAYS:
        for s in range(reach(d, 0)):
            ag_x_of(d, s).wait_send()
        for t in range(3):
            for s in range(reach(d, t)):
                ag_copy(d, s, t).wait_send()
                rs_copy(d, s + 1, t).wait_send()
    for r in range(yn):
        rx_copy(r).wait_send()
    last_x().wait_send()
    sent(ob, outer_size - 1, 0)
    sent(us, chip_size - 1, 1)
    sent(ua, chip_size - 1, 8)
    sent(tp, chip_size - 1, 2)
    sent(pm, chip_size - 1, 3)
    sent(uw, outer_size - 1, 4)
    sent(eo, outer_size - 1, 5)
    sent(tzl, zn - 1, 6)
    sent(sel, 3, 7)
    sent(tzr, zn - 1, 9)
    for copy in go_out:
        copy.wait()


def hand_over(*refs):
    count = (len(refs) - 2) // 3
    into, out, held = refs[:count], refs[count : 2 * count], refs[2 * count : 3 * count]
    come = [pltpu.make_async_copy(into[n], held[n], refs[-2].at[n]) for n in range(count)]
    leave = [pltpu.make_async_copy(held[n], out[n], refs[-1].at[n]) for n in range(count)]
    for copy in come:
        copy.start()
    for n in range(count):
        come[n].wait()
        leave[n].start()
    for copy in leave:
        copy.wait()


def on_device(hidden, down_weight, out_grad, routes, gates, omega, psi, left_old, right_old, moves):
    outer_size = lax.axis_size("outer")
    chip_size = lax.axis_size("chip")
    experts, hidden_width, columns = down_weight.shape
    model_width = columns * chip_size
    block = hidden.shape[1]
    rows_all = block * chip_size
    own = left_old.shape[1]
    rank = omega.shape[1]
    tokens = routes.shape[0]
    zn, yn = outer_size // 4, chip_size // 2
    scale_right = 10.0 / (rows_all * (hidden_width / math.sqrt(model_width) + math.sqrt(hidden_width)))
    scale_left = 10.0 / (rows_all * (model_width / math.sqrt(hidden_width) + math.sqrt(model_width)))
    far = yn // 2
    lanes = min(rows_all, 128)
    piece = experts * rank * (rows_all // lanes) // chip_size
    pay_width = experts * (columns + own)
    bf16, f32 = jnp.bfloat16, jnp.float32
    dma = pltpu.SemaphoreType.DMA
    operands = (
        hidden,
        jnp.swapaxes(down_weight, 1, 2),
        out_grad,
        routes.T,
        gates.T,
        omega.T,
        psi.T,
        jnp.swapaxes(left_old, 1, 2),
        jnp.swapaxes(right_old, 1, 2),
        moves.T,
    )
    results = (
        jax.ShapeDtypeStruct(out_grad.shape, bf16),
        jax.ShapeDtypeStruct(hidden.shape, bf16),
        jax.ShapeDtypeStruct((experts, rank, own), f32),
        jax.ShapeDtypeStruct((experts, rank, columns), f32),
    )
    done = pl.pallas_call(
        functools.partial(kernel, (outer_size, chip_size, zn, yn, scale_left, scale_right)),
        out_shape=results,
        in_specs=[pl.BlockSpec(memory_space=pl.ANY)] * len(operands),
        out_specs=(pl.BlockSpec(memory_space=pl.ANY),) * 4,
        scratch_shapes=[pltpu.VMEM(a.shape, a.dtype) for a in results + operands[:-1]]
        + [
            pltpu.SMEM(operands[-1].shape, jnp.int32),
            pltpu.VMEM((experts, rows_all, hidden_width), bf16),
            pltpu.VMEM((outer_size * block, tokens), f32),
            pltpu.VMEM((outer_size, block, columns), bf16),
            pltpu.VMEM((outer_size, block, columns), bf16),
            pltpu.VMEM((experts, rows_all, columns), bf16),
            pltpu.VMEM((experts, rows_all, hidden_width), bf16),
            pltpu.VMEM((2, far, 3, block, hidden_width), bf16),
            pltpu.VMEM((yn, block, hidden_width), bf16),
            pltpu.VMEM((block, hidden_width), bf16),
            pltpu.VMEM((outer_size, block, columns), bf16),
            pltpu.VMEM((outer_size, block, columns), bf16),
            pltpu.VMEM((chip_size, block, experts * rank), f32),
            pltpu.VMEM((chip_size, rank // 2, 2 * tokens), bf16),
            pltpu.VMEM((outer_size, block, rank), bf16),
            pltpu.VMEM((outer_size, block, rank), bf16),
            pltpu.VMEM((chip_size, piece, lanes), f32),
            pltpu.VMEM((chip_size, piece, lanes), f32),
            pltpu.VMEM((piece, lanes), f32),
            pltpu.VMEM((chip_size, piece, lanes), f32),
            pltpu.VMEM((experts, rank, columns), f32),
            pltpu.VMEM((experts, rank, own), f32),
            pltpu.VMEM((zn, rank, experts * columns), bf16),
            pltpu.VMEM((zn, rank, experts * own), bf16),
            pltpu.VMEM((3, rank, pay_width), bf16),
            pltpu.VMEM((4, rank, pay_width), bf16),
            dma((len(operands),)),
            dma((len(results),)),
            dma((2, far, 3)),
            dma((2, far, 3)),
            dma((2 + 2 * far,)),
            dma((2 + 2 * far,)),
            dma((2, far, 3)),
            dma((2, far, 3)),
            dma((yn + 1,)),
            dma((yn + 1,)),
            dma((10,)),
            dma((10,)),
        ],
        compiler_params=pltpu.CompilerParams(
            collective_id=0, has_side_effects=True, vmem_limit_bytes=64 * 2**20
        ),
        name="layer",
    )(*operands)
    mixed, hidden_grad, left_moved, right_moved = pl.pallas_call(
        hand_over,
        out_shape=results,
        in_specs=[pl.BlockSpec(memory_space=pl.ANY)] * len(results),
        out_specs=(pl.BlockSpec(memory_space=pl.ANY),) * len(results),
        scratch_shapes=[pltpu.VMEM(a.shape, a.dtype) for a in results] + [dma((len(results),))] * 2,
        name="hand_over",
    )(*done)
    return (mixed, hidden_grad, jnp.swapaxes(left_moved, 1, 2), jnp.swapaxes(right_moved, 1, 2))


def solution(mesh):
    in_specs = (
        P("outer", "chip", None),
        P("outer", None, "chip"),
        P("outer", "chip"),
        P("outer", None),
        P("outer", None),
        P("chip", None),
        P(),
        P("outer", "chip", None),
        P("outer", "chip", None),
        P(),
    )
    out_specs = (
        P("outer", "chip"),
        P("outer", "chip", None),
        P("outer", "chip", None),
        P("outer", "chip", None),
    )
    return jax.shard_map(
        on_device, mesh=mesh, in_specs=in_specs, out_specs=out_specs, check_vma=False
    )
```

```python
import functools
import math

import jax
import jax.numpy as jnp
from jax import lax
from jax.experimental import pallas as pl
from jax.experimental.pallas import tpu as pltpu
from jax.sharding import PartitionSpec as P

MESH = pl.DeviceIdType.MESH


def dot(a, b, a_dim, b_dim):
    return lax.dot_general(
        a, b, (((a_dim,), (b_dim,)), ((), ())), preferred_element_type=jnp.float32
    )


def halves(a):
    high = a.astype(jnp.bfloat16)
    return high, (a - high.astype(jnp.float32)).astype(jnp.bfloat16)


def dot_halves(a, b, b_dim):
    high, low = halves(a)
    both = dot(jnp.concatenate([high, low], axis=0), b, 1, b_dim)
    return both[: a.shape[0]] + both[a.shape[0] :]


def kernel(
    sizes,
    hid_in, wt_in, og_in, routes_in, gates_in, om_in, ps_in, left_in, right_in, moves_in,
    mixed_to, hidden_grad_to, left_to, right_to,
    mixed, hidden_grad, left_out, right_out,
    hid, wv, og, routes, gates, om, ps, left_old, right_old, moves,
    full, assign, ob, gb, grad, part, rs_in, rx_in, x_in, eo, rb,
    pm, tp, uw, ur, us, ui, uo, ua, rn, ln, tzr, tzl, sel, t2,
    in_sem, out_sem, ag_s, ag_r, agx_s, agx_r, rs_s, rs_r, rx_s, rx_r, one_s, one_r,
):
    outer_size, chip_size, zn, yn, scale_left, scale_right = sizes
    o, c = lax.axis_index("outer"), lax.axis_index("chip")
    z, sub = o // 4, o % 4
    y, xl = c // 2, c % 2
    experts, block, hidden_width = hid.shape
    columns = og.shape[1]
    rank = om.shape[0]
    rows_all = full.shape[1]
    own = left_old.shape[2]
    far = yn // 2

    barrier = pltpu.get_barrier_semaphore()

    @pl.loop(1, outer_size)
    def _(i):
        pl.semaphore_signal(barrier, inc=1, device_id=((o + i) % outer_size, c), device_id_type=MESH)

    @pl.loop(1, chip_size)
    def _(i):
        pl.semaphore_signal(barrier, inc=1, device_id=(o, (c + i) % chip_size), device_id_type=MESH)

    come_in = [
        pltpu.make_async_copy(src, dst, in_sem.at[n])
        for n, (src, dst) in enumerate(
            [
                (hid_in, hid), (routes_in, routes), (gates_in, gates), (og_in, og), (om_in, om), (ps_in, ps),
                (wt_in, wv), (left_in, left_old), (right_in, right_old), (moves_in, moves),
            ]
        )
    ]
    for copy in come_in:
        copy.start()
    go_out = [
        pltpu.make_async_copy(src, dst, out_sem.at[n])
        for n, (src, dst) in enumerate(
            [(mixed, mixed_to), (hidden_grad, hidden_grad_to), (left_out, left_to), (right_out, right_to)]
        )
    ]
    def rows(chip):
        return pl.ds(pl.multiple_of(chip * block, block), block)

    come_in[0].wait()
    for copy in come_in[1:5]:
        copy.wait()
    routes_now, gates_now = routes[...], gates[...]
    tokens = routes_now.shape[1]
    place = lax.broadcasted_iota(jnp.int32, assign.shape, 0)
    expert = lax.shift_right_logical(place, 3)
    slot = (place & 7).astype(jnp.float32)
    picked = jnp.zeros(assign.shape, jnp.float32)
    weight = jnp.zeros(assign.shape, jnp.float32)
    for p in range(routes_now.shape[0]):
        hit = routes_now[p : p + 1, :] == expert
        picked = picked + jnp.where(hit, 1.0, 0.0)
        weight = weight + jnp.where(hit, gates_now[p : p + 1, :], 0.0)
    earlier = lax.broadcasted_iota(jnp.int32, (tokens, tokens), 0) < lax.broadcasted_iota(
        jnp.int32, (tokens, tokens), 1
    )
    ranks = dot(picked.astype(jnp.bfloat16), jnp.where(earlier, 1.0, 0.0).astype(jnp.bfloat16), 1, 0)
    weight = jnp.where(ranks == slot, weight, 0.0)
    assign[...] = weight
    high, low = halves(weight)
    og_now = og[...]
    outgoing = dot(high, og_now, 1, 0) + dot(low, og_now, 1, 0)
    ob[...] = outgoing.astype(jnp.bfloat16).reshape(ob.shape)
    gb[o] = ob[o]


    pl.semaphore_wait(barrier, outer_size + chip_size - 2)

    def remote(src, dst, send, recv, device):
        return pltpu.make_async_remote_copy(
            src_ref=src, dst_ref=dst, send_sem=send, recv_sem=recv, device_id=device, device_id_type=MESH
        )

    x_partner = (o, 2 * y + 1 - xl)

    def around(steps):
        return (y + steps + 2 * yn) % yn

    EXPERT = (1, 0, 0)
    FAR_WAY = (1, -1, 1)
    WAYS = (1, -1)

    def reach(d, t):
        return far if d == FAR_WAY[t] else far - 1

    def chip_of(y_at, t):
        return 2 * y_at + (1 - xl if t == 2 else xl)

    def ag_copy(d, s, t):
        source = rows(chip_of(around(-d * s), t))
        k = EXPERT[t]
        src = hid.at[k] if s == 0 and t < 2 else full.at[k, source]
        n = WAYS.index(d)
        return remote(
            src, full.at[k, source], ag_s.at[n, s, t], ag_r.at[n, s, t], (o, 2 * around(d) + xl)
        )

    def ag_x(n, k, y_at):
        source = rows(2 * y_at + xl)
        src = hid.at[k] if n < 2 else full.at[k, source]
        return remote(src, full.at[k, source], agx_s.at[n], agx_r.at[n], x_partner)

    def ag_x_of(d, s):
        return ag_x(2 + WAYS.index(d) * far + s, 1, around(-d * (s + 1)))

    def ag_step(s):
        for t in range(3):
            for d in WAYS:
                if s < reach(d, t):
                    ag_copy(d, s, t).wait_recv()
                    if s + 1 < reach(d, t):
                        ag_copy(d, s + 1, t).start()
                    if t == 0:
                        ag_x_of(d, s).start()

    ag_x(0, 0, y).start()
    for t in range(2):
        for d in WAYS:
            if reach(d, t):
                ag_copy(d, 0, t).start()
    ag_x(1, 1, y).start()

    def spread(src_of, dst, number, axis_size, device_of):
        @pl.loop(1, axis_size)
        def _(i):
            remote(src_of(i), dst, one_s.at[number], one_r.at[number], device_of(i)).start()

    def arrived(buf, count, number):
        ref = buf.at[pl.ds(0, count)]
        pltpu.make_async_copy(ref, ref, one_r.at[number]).wait()

    def sent(buf, count, number):
        ref = buf.at[pl.ds(0, count)]
        pltpu.make_async_copy(ref, ref, one_s.at[number]).wait()

    def other_group(i):
        return (o + i) % outer_size

    def other_chip(i):
        return (c + i) % chip_size

    spread(lambda i: ob.at[other_group(i)], gb.at[o], 0, outer_size, lambda i: (other_group(i), c))

    token_cols = dot_halves(om[...], og_now, 1)
    fold = rank // 2
    tp[c] = jnp.concatenate([token_cols[:fold], token_cols[fold:]], axis=1).astype(jnp.bfloat16)
    spread(lambda i: tp.at[c], tp.at[c], 2, chip_size, lambda i: (o, other_chip(i)))

    for copy in come_in[5:]:
        copy.wait()
    for k in range(experts):
        full[k, rows(c), :] = hid[k]
    psi_high, psi_low = halves(ps[...])
    pm[c] = jnp.concatenate([dot(hid[k], psi_high, 1, 1) + dot(hid[k], psi_low, 1, 1) for k in range(experts)], axis=1)
    spread(lambda i: pm.at[c], pm.at[c], 3, chip_size, lambda i: (o, other_chip(i)))

    ag_x(0, 0, y).wait_recv()
    for d in WAYS:
        if reach(d, 2):
            ag_copy(d, 0, 2).start()
    for s in range(far - 1):
        ag_step(s)

    arrived(tp, chip_size - 1, 2)
    token_cols = jnp.sum(tp[...].astype(jnp.float32), axis=0)
    token_cols = jnp.concatenate([token_cols[:, :tokens], token_cols[:, tokens:]], axis=0)
    uw[...] = dot_halves(assign[...], token_cols.astype(jnp.bfloat16), 1).astype(jnp.bfloat16).reshape(uw.shape)
    ur[o] = uw[o]
    spread(lambda i: uw.at[other_group(i)], ur.at[o], 4, outer_size, lambda i: (other_group(i), c))

    arrived(gb, outer_size - 1, 0)
    eight = block // experts
    come = gb[...].astype(jnp.float32)
    for k in range(experts):
        grad[k] = come[:, k * eight : (k + 1) * eight, :].reshape(rows_all, columns).astype(jnp.bfloat16)

    lanes = us.shape[2]
    lane_cuts = rows_all // lanes
    piece = us.shape[1]

    def sum_send(parts, send, into, number):
        both = jnp.concatenate(parts, axis=0)
        for p in range(chip_size):
            at, cut = p // lane_cuts, p % lane_cuts
            send[p] = both[at * piece : (at + 1) * piece, cut * lanes : (cut + 1) * lanes]
        into[c] = send[c]
        spread(lambda i: send.at[other_chip(i)], into.at[c], number, chip_size, lambda i: (o, other_chip(i)))

    def sum_share(into, own_sum, full_sum, number):
        arrived(into, chip_size - 1, number)
        own_sum[...] = jnp.sum(into[...], axis=0)
        full_sum[c] = own_sum[...]
        spread(lambda i: own_sum, full_sum.at[c], 8, chip_size, lambda i: (o, other_chip(i)))

    def sum_take(full_sum):
        arrived(full_sum, chip_size - 1, 8)
        lines = []
        for at in range(chip_size // lane_cuts):
            lines.append(
                jnp.concatenate([full_sum[at * lane_cuts + cut] for cut in range(lane_cuts)], axis=1)
            )
        return jnp.concatenate(lines, axis=0)

    sums = []
    arrived(pm, chip_size - 1, 3)
    row_psi = pm[...].reshape(rows_all, experts * rank)
    psi_high, psi_low = halves(row_psi)
    for k in range(experts):
        both = jnp.concatenate([psi_high[:, k * rank : (k + 1) * rank], psi_low[:, k * rank : (k + 1) * rank]], axis=1)
        both = dot(both, grad[k], 0, 0)
        sums.append(dot_halves(both[:rank] + both[rank:], grad[k], 1))
    sum_send(sums, us, ui, 1)

    tile = min(512, hidden_width)

    def partial_of(k):
        @pl.loop(0, hidden_width // tile)
        def _(n):
            cut = pl.ds(pl.multiple_of(n * tile, tile), tile)
            part[k, :, cut] = dot(grad[k], wv[k, :, cut], 1, 0).astype(jnp.bfloat16)

    def rs_rows(d, m, t):
        return rows(chip_of(around(d * m), t))

    def rs_copy(d, m, t):
        n = WAYS.index(d)
        return remote(
            part.at[EXPERT[t], rs_rows(d, m, t)],
            rs_in.at[n, m - 1, t],
            rs_s.at[n, m - 1, t],
            rs_r.at[n, m - 1, t],
            (o, 2 * around(d) + xl),
        )

    def rx_copy(r):
        src = part.at[1, rows(2 * around(r) + 1 - xl)]
        return remote(src, rx_in.at[r], rx_s.at[r], rx_r.at[r], x_partner)

    def rx_add(r):
        rx_copy(r).wait_recv()
        at = rows(2 * around(r) + xl)
        part[1, at, :] = (part[1, at, :].astype(jnp.float32) + rx_in[r].astype(jnp.float32)).astype(jnp.bfloat16)

    def rs_start(d, t):
        if t == 0:
            rx_add(d * reach(d, t) % yn)
        rs_copy(d, reach(d, t), t).start()

    def rs_first(t):
        for d in WAYS:
            if reach(d, t):
                rs_start(d, t)

    def rs_relay(d, m, t):
        if t == 0:
            rx_add(d * m % yn)
        rs_copy(d, m + 1, t).wait_recv()
        at = rs_rows(d, m, t)
        total = part[EXPERT[t], at, :].astype(jnp.float32) + rs_in[WAYS.index(d), m, t].astype(jnp.float32)
        part[EXPERT[t], at, :] = total.astype(jnp.bfloat16)
        rs_copy(d, m, t).start()

    todo = []
    for m in range(far - 1, 0, -1):
        for t in (1, 2, 0):
            if t == 0 and m == far - 1:
                todo += [functools.partial(rs_start, d, 0) for d in WAYS if reach(d, 0)]
            for d in WAYS:
                if m < reach(d, t):
                    todo.append(functools.partial(rs_relay, d, m, t))
    if far == 1:
        todo += [functools.partial(rs_start, d, 0) for d in WAYS if reach(d, 0)]

    def rs_do(count):
        for _ in range(min(count, len(todo))):
            todo.pop(0)()

    def rs_total(t):
        total = part[EXPERT[t], rs_rows(1, 0, t), :].astype(jnp.float32)
        for d in WAYS:
            if reach(d, t):
                rs_copy(d, 1, t).wait_recv()
                total = total + rs_in[WAYS.index(d), 0, t].astype(jnp.float32)
        return total

    def last_x():
        return remote(part.at[0, rs_rows(1, 0, 2)], x_in, rx_s.at[yn], rx_r.at[yn], x_partner)

    partial_of(0)
    rs_first(1)
    rs_first(2)
    ag_step(far - 1)
    partial_of(1)
    order = sorted(range(yn), key=lambda r: -min(r, yn - r))
    for r in order:
        rx_copy(r).start()
    ag_x(1, 1, y).wait_recv()
    for d in WAYS:
        for s in range(reach(d, 0)):
            ag_x_of(d, s).wait_recv()

    outputs = []
    for k in range(experts):
        outputs.append(dot(full[k], wv[k], 1, 1).reshape(outer_size, eight, columns))
    eo[...] = jnp.concatenate(outputs, axis=1).astype(jnp.bfloat16)
    rb[o] = eo[o]
    spread(lambda i: eo.at[other_group(i)], rb.at[o], 5, outer_size, lambda i: (other_group(i), c))
    rs_do(5)
    arrived(ur, outer_size - 1, 4)
    cols = ur[...].astype(jnp.float32)
    for k in range(experts):
        row_cols = cols[:, k * eight : (k + 1) * eight, :].reshape(rows_all, rank).astype(jnp.bfloat16)
        sketch = dot(row_cols, full[k], 0, 0)
        row_width = dot_halves(sketch, full[k], 1)
        rn[k] = 0.5 * right_old[k] + 0.5 * scale_right * dot_halves(row_width, grad[k], 0)
        tzr[z, :, k * columns : (k + 1) * columns] = rn[k].astype(jnp.bfloat16)
    spread(lambda i: tzr.at[z], tzr.at[z], 9, zn, lambda i: (((z + i) % zn) * 4 + sub, c))
    sum_share(ui, uo, ua, 1)
    rs_do(6)

    sums = sum_take(ua)
    mine = pl.ds(pl.multiple_of(c * own, own), own)
    for k in range(experts):
        row_left = sums[k * rank : (k + 1) * rank]
        ln[k] = 0.5 * left_old[k] + 0.5 * scale_left * dot_halves(row_left, full[k, :, mine], 0)
        tzl[z, :, k * own : (k + 1) * own] = ln[k].astype(jnp.bfloat16)
    spread(lambda i: tzl.at[z], tzl.at[z], 6, zn, lambda i: (((z + i) % zn) * 4 + sub, c))

    def source_of(group):
        source = group
        for m in range(moves.shape[1]):
            a, b = moves[0, m], moves[1, m]
            source = jnp.where(group == a, b, jnp.where(group == b, a, source))
        return source

    rs_do(6)
    part[0, rs_rows(1, 0, 2), :] = rs_total(2).astype(jnp.bfloat16)
    last_x().start()
    arrived(tzr, zn - 1, 9)

    right_width = experts * columns
    arrived(tzl, zn - 1, 6)
    for i in range(1, 4):
        at = lax.shift_right_logical(source_of(z * 4 + (sub + i) % 4), 2)
        sel[i - 1, :, :right_width] = tzr[at]
        sel[i - 1, :, right_width:] = tzl[at]
        remote(
            sel.at[i - 1], t2.at[sub], one_s.at[7], one_r.at[7], (z * 4 + (sub + i) % 4, c)
        ).start()
    mine_from = source_of(o)
    at = lax.shift_right_logical(mine_from, 2)
    t2[sub, :, :right_width] = tzr[at]
    t2[sub, :, right_width:] = tzl[at]

    rx_add(0)
    hidden_grad[1] = rs_total(0).astype(jnp.bfloat16)
    total = rs_total(1)

    arrived(rb, outer_size - 1, 5)
    back = rb[...].reshape(outer_size * block, columns)
    high, low = halves(assign[...])
    mixed[...] = (dot(high, back, 0, 0) + dot(low, back, 0, 0)).astype(jnp.bfloat16)

    go_out[0].start()
    last_x().wait_recv()
    hidden_grad[0] = (total + x_in[...].astype(jnp.float32)).astype(jnp.bfloat16)

    go_out[1].start()
    stays = mine_from == o
    arrived(t2, 3, 7)
    came = t2[mine_from & 3].astype(jnp.float32)
    for k in range(experts):
        right_out[k] = jnp.where(stays, rn[k], came[:, k * columns : (k + 1) * columns])
        at = right_width + k * own
        left_out[k] = jnp.where(stays, ln[k], came[:, at : at + own])

    go_out[2].start()
    go_out[3].start()

    ag_x(0, 0, y).wait_send()
    ag_x(1, 1, y).wait_send()
    for d in WAYS:
        for s in range(reach(d, 0)):
            ag_x_of(d, s).wait_send()
        for t in range(3):
            for s in range(reach(d, t)):
                ag_copy(d, s, t).wait_send()
                rs_copy(d, s + 1, t).wait_send()
    for r in range(yn):
        rx_copy(r).wait_send()
    last_x().wait_send()
    sent(ob, outer_size - 1, 0)
    sent(us, chip_size - 1, 1)
    sent(ua, chip_size - 1, 8)
    sent(tp, chip_size - 1, 2)
    sent(pm, chip_size - 1, 3)
    sent(uw, outer_size - 1, 4)
    sent(eo, outer_size - 1, 5)
    sent(tzl, zn - 1, 6)
    sent(sel, 3, 7)
    sent(tzr, zn - 1, 9)
    for copy in go_out:
        copy.wait()


def hand_over(*refs):
    count = (len(refs) - 2) // 3
    into, out, held = refs[:count], refs[count : 2 * count], refs[2 * count : 3 * count]
    come = [pltpu.make_async_copy(into[n], held[n], refs[-2].at[n]) for n in range(count)]
    leave = [pltpu.make_async_copy(held[n], out[n], refs[-1].at[n]) for n in range(count)]
    for copy in come:
        copy.start()
    for n in range(count):
        come[n].wait()
        leave[n].start()
    for copy in leave:
        copy.wait()


def on_device(hidden, down_weight, out_grad, routes, gates, omega, psi, left_old, right_old, moves):
    outer_size = lax.axis_size("outer")
    chip_size = lax.axis_size("chip")
    experts, hidden_width, columns = down_weight.shape
    model_width = columns * chip_size
    block = hidden.shape[1]
    rows_all = block * chip_size
    own = left_old.shape[1]
    rank = omega.shape[1]
    tokens = routes.shape[0]
    zn, yn = outer_size // 4, chip_size // 2
    scale_right = 10.0 / (rows_all * (hidden_width / math.sqrt(model_width) + math.sqrt(hidden_width)))
    scale_left = 10.0 / (rows_all * (model_width / math.sqrt(hidden_width) + math.sqrt(model_width)))
    far = yn // 2
    lanes = min(rows_all, 128)
    piece = experts * rank * (rows_all // lanes) // chip_size
    pay_width = experts * (columns + own)
    bf16, f32 = jnp.bfloat16, jnp.float32
    dma = pltpu.SemaphoreType.DMA
    operands = (
        hidden,
        jnp.swapaxes(down_weight, 1, 2),
        out_grad,
        routes.T,
        gates.T,
        omega.T,
        psi.T,
        jnp.swapaxes(left_old, 1, 2),
        jnp.swapaxes(right_old, 1, 2),
        moves.T,
    )
    results = (
        jax.ShapeDtypeStruct(out_grad.shape, bf16),
        jax.ShapeDtypeStruct(hidden.shape, bf16),
        jax.ShapeDtypeStruct((experts, rank, own), f32),
        jax.ShapeDtypeStruct((experts, rank, columns), f32),
    )
    done = pl.pallas_call(
        functools.partial(kernel, (outer_size, chip_size, zn, yn, scale_left, scale_right)),
        out_shape=results,
        in_specs=[pl.BlockSpec(memory_space=pl.ANY)] * len(operands),
        out_specs=(pl.BlockSpec(memory_space=pl.ANY),) * 4,
        scratch_shapes=[pltpu.VMEM(a.shape, a.dtype) for a in results + operands[:-1]]
        + [
            pltpu.SMEM(operands[-1].shape, jnp.int32),
            pltpu.VMEM((experts, rows_all, hidden_width), bf16),
            pltpu.VMEM((outer_size * block, tokens), f32),
            pltpu.VMEM((outer_size, block, columns), bf16),
            pltpu.VMEM((outer_size, block, columns), bf16),
            pltpu.VMEM((experts, rows_all, columns), bf16),
            pltpu.VMEM((experts, rows_all, hidden_width), bf16),
            pltpu.VMEM((2, far, 3, block, hidden_width), bf16),
            pltpu.VMEM((yn, block, hidden_width), bf16),
            pltpu.VMEM((block, hidden_width), bf16),
            pltpu.VMEM((outer_size, block, columns), bf16),
            pltpu.VMEM((outer_size, block, columns), bf16),
            pltpu.VMEM((chip_size, block, experts * rank), f32),
            pltpu.VMEM((chip_size, rank // 2, 2 * tokens), bf16),
            pltpu.VMEM((outer_size, block, rank), bf16),
            pltpu.VMEM((outer_size, block, rank), bf16),
            pltpu.VMEM((chip_size, piece, lanes), f32),
            pltpu.VMEM((chip_size, piece, lanes), f32),
            pltpu.VMEM((piece, lanes), f32),
            pltpu.VMEM((chip_size, piece, lanes), f32),
            pltpu.VMEM((experts, rank, columns), f32),
            pltpu.VMEM((experts, rank, own), f32),
            pltpu.VMEM((zn, rank, experts * columns), bf16),
            pltpu.VMEM((zn, rank, experts * own), bf16),
            pltpu.VMEM((3, rank, pay_width), bf16),
            pltpu.VMEM((4, rank, pay_width), bf16),
            dma((len(operands),)),
            dma((len(results),)),
            dma((2, far, 3)),
            dma((2, far, 3)),
            dma((2 + 2 * far,)),
            dma((2 + 2 * far,)),
            dma((2, far, 3)),
            dma((2, far, 3)),
            dma((yn + 1,)),
            dma((yn + 1,)),
            dma((10,)),
            dma((10,)),
        ],
        compiler_params=pltpu.CompilerParams(
            collective_id=0, has_side_effects=True, vmem_limit_bytes=64 * 2**20
        ),
        name="layer",
    )(*operands)
    mixed, hidden_grad, left_moved, right_moved = pl.pallas_call(
        hand_over,
        out_shape=results,
        in_specs=[pl.BlockSpec(memory_space=pl.ANY)] * len(results),
        out_specs=(pl.BlockSpec(memory_space=pl.ANY),) * len(results),
        scratch_shapes=[pltpu.VMEM(a.shape, a.dtype) for a in results] + [dma((len(results),))] * 2,
        name="hand_over",
    )(*done)
    return (mixed, hidden_grad, jnp.swapaxes(left_moved, 1, 2), jnp.swapaxes(right_moved, 1, 2))


def solution(mesh):
    in_specs = (
        P("outer", "chip", None),
        P("outer", None, "chip"),
        P("outer", "chip"),
        P("outer", None),
        P("outer", None),
        P("chip", None),
        P(),
        P("outer", "chip", None),
        P("outer", "chip", None),
        P(),
    )
    out_specs = (
        P("outer", "chip"),
        P("outer", "chip", None),
        P("outer", "chip", None),
        P("outer", "chip", None),
    )
    return jax.shard_map(
        on_device, mesh=mesh, in_specs=in_specs, out_specs=out_specs, check_vma=False
    )
```
